512 devices in a mesh: lat: 32 (over z, core), ens: 16 (over x, y).
Axes of the slice: x: 4, y: 4, z: 16, core: 2. Of those that a mesh axis runs over, the one named last changes fastest.
Arguments:
- inputs: bfloat16 [16, 32, 720, 256], P('ens', 'lat'), may hold values from -6 to 6
- cotangent: bfloat16 [16, 32, 720, 256], P('ens', 'lat'), may hold values from -6 to 6
- weights: bfloat16 [4, 256, 256], replicated, may hold values from -0.1875 to 0.1875
- cycle_offsets: int32 [32, 16], P('lat'), may hold values from -1 to 1
- lon_shifts: int32 [32, 16], P('lat'), may hold values from 0 to 719
- basis_ids: int32 [32, 16], P('lat'), may hold values from 0 to 3
- entry_values: bfloat16 [32, 16], P('lat'), may hold values from 0.099609375 to 1
Outputs:
- activations: bfloat16 [16, 32, 720, 256], P('ens', 'lat')
- grad_inputs: bfloat16 [16, 32, 720, 256], P('ens', 'lat')
- grad_weights: float32 [4, 256, 256], replicated
The draws below stay inside these ranges and needn't reach their ends.
Inputs may be any that keep to these rules, and one draw needn't show every extreme that they name: `cycle_offsets`: an entry's cycle lies at most 1 cycle from its output cycle.
All inputs are finite; a program needn't handle non-finite values.
Results may differ from the reference program's by a relative error of at most 0.0063.
Values may be sent and summed in bfloat16 or wider, within the bound.
No kernel may reach another device: no remote copies, remote signals or barrier semaphores. Data moves between devices by JAX's collectives and lax.ppermute only.
A program may use at most 192 MiB of HBM per device.

```python
import math
import jax
import jax.numpy as jnp
from jax import lax

L = 720
C = 256
K = 4
NE = 16
H = 1
NLAT = 32
MEMBERS = 16


def place_ends(array, own_key, low, largest):
    longest = array.shape.index(max(array.shape))
    spots = []
    for shift in (0, 1):
        where = [jax.random.randint(jax.random.fold_in(own_key, axis), (), 0, length) for axis, length in enumerate(array.shape)]
        where[longest] = (where[longest] + shift) % array.shape[longest]
        spots.append(tuple(where))
    return array.at[spots[0]].set(low).at[spots[1]].set(largest)


def steps_of(stream_key, extent, pieces, smallest, largest):
    def one(axis_at, shards_of):
        steps = jax.random.uniform(jax.random.fold_in(jax.random.fold_in(stream_key, 6), axis_at), (shards_of,), jnp.float32, smallest / len(pieces), largest / len(pieces))
        return jnp.repeat(jnp.exp(steps), extent[axis_at] // shards_of).reshape((-1,) + (1,) * (len(extent) - axis_at - 1))

    loudness = one(*pieces[0])
    for cut in pieces[1:]:
        loudness = loudness * one(*cut)
    return loudness


def bell_draw(own_key, shape, width, reach, cuts=(), held_as=jnp.bfloat16):
    array = width * jax.random.normal(own_key, shape, jnp.float32)
    if cuts:
        array = array * steps_of(own_key, shape, cuts, -0.22, 0.18)
    return jnp.clip(array, -reach, reach).astype(held_as)


def setup_inputs(seed: int = 0) -> dict:
    key_of = jax.random.split(jax.random.key(seed), 8)
    inputs = bell_draw(key_of[0], (MEMBERS, NLAT, L, C), 1.0, 6.0, ((0, 16), (1, 32)))
    cotangent = bell_draw(key_of[1], (MEMBERS, NLAT, L, C), 1.0, 6.0, ((0, 16), (1, 32)))
    weights = bell_draw(key_of[2], (K, C, C), (K * C) ** -0.5, 0.1875)
    cycle_offsets = place_ends(jax.random.randint(key_of[3], (NLAT, NE), 0 - H, H + 1), jax.random.fold_in(key_of[3], 1), 0 - H, H).astype(jnp.int32)
    lon_shifts = place_ends(jax.random.randint(key_of[4], (NLAT, NE), 0, L), jax.random.fold_in(key_of[4], 1), 0, L - 1).astype(jnp.int32)
    basis_ids = place_ends(jax.random.randint(key_of[5], (NLAT, NE), 0, K), jax.random.fold_in(key_of[5], 1), 0, K - 1).astype(jnp.int32)
    entry_values = jnp.clip(0.099609375 + 0.9003906 * jax.random.uniform(key_of[6], (NLAT, NE), jnp.float32) ** steps_of(key_of[6], (NLAT, NE), ((0, 32),), -0.2, 0.2), 0.099609375, 1.0).astype(jnp.bfloat16)
    return dict(inputs=inputs, cotangent=cotangent, weights=weights, cycle_offsets=cycle_offsets, lon_shifts=lon_shifts, basis_ids=basis_ids, entry_values=entry_values)


def spread_cycles(field_wide, cycle_offsets, lon_shifts, basis_ids, entry_values):
    padded = jnp.pad(field_wide, ((H, H), (0, 0), (0, 0)))
    lon_index = jnp.arange(L, dtype=jnp.int32)
    basis_index = jnp.arange(K, dtype=jnp.int32)

    def per_cycle(cycle_now):
        source = cycle_now + H + cycle_offsets[cycle_now]
        columns = (lon_index[None, :] + lon_shifts[cycle_now][:, None]) % L
        latitude_slab_rows = padded[source[:, None], columns]
        channel_mixing = entry_values[cycle_now].astype(jnp.float32)[:, None] * (basis_ids[cycle_now][:, None] == basis_index[None, :]).astype(jnp.float32)
        return jnp.einsum('ek,elc->lkc', channel_mixing, latitude_slab_rows)
    return lax.map(per_cycle, jnp.arange(NLAT, dtype=jnp.int32))

def collect_latitude_cycles(grad_wide, cycle_offsets, lon_shifts, basis_ids, entry_values):
    lon_index = jnp.arange(L, dtype=jnp.int32)

    def step_forward(summed, cycle_now):
        columns = (lon_index[None, :] - lon_shifts[cycle_now][:, None]) % L
        latitude_slab_rows = grad_wide[cycle_now][columns, basis_ids[cycle_now][:, None]]
        scaled_rows = entry_values[cycle_now].astype(jnp.float32)[:, None, None] * latitude_slab_rows
        target = cycle_now + H + cycle_offsets[cycle_now]
        return (summed.at[target].add(scaled_rows), None)
    start = jnp.zeros((NLAT + 2 * H, L, C), jnp.float32)
    summed = lax.scan(step_forward, start, jnp.arange(NLAT, dtype=jnp.int32))[0]
    return summed[H:H + NLAT]

def reference(inputs, cotangent, weights, cycle_offsets, lon_shifts, basis_ids, entry_values):
    flat_weights = weights.reshape(K * C, C)

    def member(summed, pair):
        field_now, grad_now = pair
        basis_wide = spread_cycles(field_now.astype(jnp.float32), cycle_offsets, lon_shifts, basis_ids, entry_values)
        flat_basis = basis_wide.astype(jnp.bfloat16).reshape(NLAT * L, K * C)
        preact = jnp.dot(flat_basis, flat_weights, preferred_element_type=jnp.float32)
        activated, gelu_back = jax.vjp(jax.nn.gelu, preact)
        grad_pre = gelu_back(grad_now.reshape(NLAT * L, C).astype(jnp.float32))[0].astype(jnp.bfloat16)
        grad_flat = jnp.dot(grad_pre, flat_weights.T, preferred_element_type=jnp.float32).astype(jnp.bfloat16)
        field_gradient = collect_latitude_cycles(grad_flat.reshape(NLAT, L, K, C).astype(jnp.float32), cycle_offsets, lon_shifts, basis_ids, entry_values)
        partial_w = jnp.dot(flat_basis.T, grad_pre, preferred_element_type=jnp.float32)
        return (summed + partial_w, (activated.astype(jnp.bfloat16).reshape(NLAT, L, C), field_gradient.astype(jnp.bfloat16)))
    summed, stacked = lax.scan(member, jnp.zeros((K * C, C), jnp.float32), (inputs, cotangent))
    grad_weights = (summed * (1.0 / math.sqrt(MEMBERS * NLAT * L))).reshape(K, C, C)
    return (stacked[0], stacked[1], grad_weights)
```

```python
import functools
import math

import jax
import jax.numpy as jnp
import numpy as np
from jax import lax
from jax.experimental import pallas as pl
from jax.experimental.pallas import tpu as pltpu
from jax.sharding import Mesh
from jax.sharding import PartitionSpec as P

BF16 = jnp.bfloat16
F32 = jnp.float32
LANES = 128
SLAB = 48
VMEM_BYTES = 48 * 1024 * 1024
LAT = ("za", "zp", "core")
ENS = ("x", "y")
NEAR = ("zp", "core", "x", "y")
FAR = ("za",)


def along(axis, distance):
    devices = range(lax.axis_size(axis))
    return [(i - distance, i) for i in devices if i - distance in devices]


def fill_twice(slabs, slot, field):
    lon_count = field.shape[0]
    for half in range(field.shape[1] // LANES):
        part = field[:, half * LANES : (half + 1) * LANES]
        slabs[slot + half, 0:lon_count, :] = part
        slabs[slot + half, lon_count : 2 * lon_count, :] = part


def forward_kernel(
    offsets, shifts, basis_ids, values, below, own, above, weights, cotangent,
    activated, grad_pre, partial_w, slabs, summed, basis, preact,
):
    lon_count, channels = own.shape
    halves = channels // LANES
    basis_count = weights.shape[0] // channels
    for slot, field in enumerate((below, own, above)):
        fill_twice(slabs, slot * halves, field[...].astype(F32))
    summed[...] = jnp.zeros_like(summed)

    def add_entry(entry, carry):
        source = (offsets[0, entry] + 1) * halves
        target = basis_ids[0, entry] * halves
        shift = shifts[0, entry]
        value = values[0, entry]
        for half in range(halves):
            summed[target + half] += value * slabs[source + half, pl.ds(shift, lon_count), :]
        return carry

    lax.fori_loop(0, offsets.shape[1], add_entry, 0)
    for column in range(basis_count * halves):
        basis[:, column * LANES : (column + 1) * LANES] = summed[column].astype(BF16)
    preact[...] = jnp.dot(basis[...], weights[...], preferred_element_type=F32)

    def gelu_rows(step, carry):
        rows = pl.ds(pl.multiple_of(step * SLAB, SLAB), SLAB)
        v = preact[rows, :]
        root = math.sqrt(2.0 / math.pi)
        square = v * v
        bent = jnp.tanh(root * (v + 0.044715 * (v * square)))
        activated[rows, :] = (0.5 * v * (1.0 + bent)).astype(BF16)
        slope = 0.5 * (1.0 + bent) + 0.5 * v * (1.0 - bent * bent) * (
            root * (1.0 + (3.0 * 0.044715) * square)
        )
        grad_pre[rows, :] = (cotangent[rows, :].astype(F32) * slope).astype(BF16)
        return carry

    lax.fori_loop(0, lon_count // SLAB, gelu_rows, 0)
    partial_w[...] = lax.dot_general(
        basis[...], grad_pre[...], (((0,), (0,)), ((), ())), preferred_element_type=F32
    ).astype(BF16)


def backward_kernel(
    offsets, shifts, basis_ids, values, grad_pre, weights, down, own, up, slabs, summed,
):
    lon_count, channels = grad_pre.shape
    halves = channels // LANES
    basis_count = weights.shape[0] // channels
    for k in range(basis_count):
        product = lax.dot_general(
            grad_pre[...],
            weights[k * channels : (k + 1) * channels, :],
            (((1,), (1,)), ((), ())),
            preferred_element_type=F32,
        )
        fill_twice(slabs, k * halves, product.astype(BF16).astype(F32))
    summed[...] = jnp.zeros_like(summed)

    def add_entry(entry, carry):
        target = (offsets[0, entry] + 1) * halves
        source = basis_ids[0, entry] * halves
        start = lon_count - shifts[0, entry]
        value = values[0, entry]
        for half in range(halves):
            summed[target + half] += value * slabs[source + half, pl.ds(start, lon_count), :]
        return carry

    lax.fori_loop(0, offsets.shape[1], add_entry, 0)
    for slot, out in enumerate((down, own, up)):
        for half in range(halves):
            out[:, half * LANES : (half + 1) * LANES] = summed[slot * halves + half].astype(out.dtype)


def specs(scalars, arrays):
    return [pl.BlockSpec(memory_space=pltpu.SMEM)] * scalars + [
        pl.BlockSpec(memory_space=pltpu.VMEM)
    ] * arrays


def forward(tables, below, own, above, weights, cotangent):
    lon_count, channels = own.shape
    halves = channels // LANES
    wide = weights.shape[0]
    return pl.pallas_call(
        forward_kernel,
        out_shape=(
            jax.ShapeDtypeStruct((lon_count, channels), BF16),
            jax.ShapeDtypeStruct((lon_count, channels), BF16),
            jax.ShapeDtypeStruct((wide, channels), BF16),
        ),
        in_specs=specs(4, 5),
        out_specs=tuple(specs(0, 3)),
        scratch_shapes=[
            pltpu.VMEM((3 * halves, 2 * lon_count, LANES), F32),
            pltpu.VMEM((wide // LANES, lon_count, LANES), F32),
            pltpu.VMEM((lon_count, wide), BF16),
            pltpu.VMEM((lon_count, channels), F32),
        ],
        compiler_params=pltpu.CompilerParams(vmem_limit_bytes=VMEM_BYTES),
        cost_estimate=pl.CostEstimate(
            flops=4 * lon_count * wide * channels, bytes_accessed=16 * 1024 * 1024, transcendentals=0
        ),
        name="conv_forward",
    )(*tables, below, own, above, weights, cotangent)


def backward(tables, grad_pre, weights):
    lon_count, channels = grad_pre.shape
    halves = channels // LANES
    wide = weights.shape[0]
    return pl.pallas_call(
        backward_kernel,
        out_shape=(
            jax.ShapeDtypeStruct((lon_count, channels), BF16),
            jax.ShapeDtypeStruct((lon_count, channels), F32),
            jax.ShapeDtypeStruct((lon_count, channels), BF16),
        ),
        in_specs=specs(4, 2),
        out_specs=tuple(specs(0, 3)),
        scratch_shapes=[
            pltpu.VMEM((wide // LANES, 2 * lon_count, LANES), F32),
            pltpu.VMEM((3 * halves, lon_count, LANES), F32),
        ],
        compiler_params=pltpu.CompilerParams(vmem_limit_bytes=VMEM_BYTES),
        cost_estimate=pl.CostEstimate(
            flops=2 * lon_count * wide * channels, bytes_accessed=16 * 1024 * 1024, transcendentals=0
        ),
        name="conv_backward",
    )(*tables, grad_pre, weights)


def gathered(block, axes):
    count = lax.axis_size(axes)
    return lax.all_to_all(jnp.broadcast_to(block[None], (count,) + block.shape), axes, 0, 0)


def on_device(inputs, cotangent, weights, cycle_offsets, lon_shifts, basis_ids, entry_values):
    own = inputs[0, 0]
    lon_count, channels = own.shape
    basis_count = weights.shape[0]
    flat_weights = weights.reshape(basis_count * channels, channels)
    tables = (cycle_offsets, lon_shifts, basis_ids, entry_values.astype(F32))
    below = lax.ppermute(own, LAT, along(LAT, 1))
    above = lax.ppermute(own, LAT, along(LAT, -1))
    activated, grad_pre, partial_w = forward(
        tables, below, own, above, flat_weights, cotangent[0, 0]
    )
    near = lax.axis_size(NEAR)
    pieces = lax.all_to_all(partial_w.reshape(near, -1, channels), NEAR, 0, 0)
    chunk = pieces.astype(F32).sum(0).astype(BF16)

    down, middle, up = backward(tables, grad_pre, flat_weights)
    from_above = lax.ppermute(up, LAT, along(LAT, 1))
    from_below = lax.ppermute(down, LAT, along(LAT, -1))
    field_gradient = (middle + from_above.astype(F32) + from_below.astype(F32)).astype(BF16)

    cell_count = lax.axis_size(LAT) * lax.axis_size(ENS) * lon_count
    total = gathered(chunk, FAR).astype(F32).sum(0) * (1.0 / math.sqrt(cell_count))
    whole = gathered(total.astype(BF16), NEAR)
    grad_weights = whole.reshape(basis_count, channels, channels).astype(F32)
    return (activated[None, None], field_gradient[None, None], grad_weights)


def solution(mesh):
    lat_count, ens_count = mesh.devices.shape
    grid = Mesh(
        np.asarray(mesh.devices).reshape(lat_count // 4, 2, 2, 4, ens_count // 4),
        LAT + ENS,
    )
    placed = (
        P(ENS, LAT, None, None),
        P(ENS, LAT, None, None),
        P(),
        P(LAT, None),
        P(LAT, None),
        P(LAT, None),
        P(LAT, None),
    )
    return jax.shard_map(
        on_device,
        mesh=grid,
        in_specs=placed,
        out_specs=(P(ENS, LAT, None, None), P(ENS, LAT, None, None), P()),
        check_vma=False,
    )
```

```python
import functools
import math

import jax
import jax.numpy as jnp
import numpy as np
from jax import lax
from jax.experimental import pallas as pl
from jax.experimental.pallas import tpu as pltpu
from jax.sharding import Mesh
from jax.sharding import PartitionSpec as P

BF16 = jnp.bfloat16
F32 = jnp.float32
LANES = 128
SLAB = 48
VMEM_BYTES = 48 * 1024 * 1024
LAT = ("za", "zp", "core")
ENS = ("x", "y")
NEAR = ("zp", "core", "x", "y")
FAR = ("za",)


def pair_swap(axis, first):
    devices = range(lax.axis_size(axis))
    pairs = [(i, i + 1) for i in devices if i % 2 == first and i + 1 in devices]
    return pairs + [(j, i) for i, j in pairs]


def fill_twice(slabs, slot, field):
    lon_count = field.shape[0]
    for half in range(field.shape[1] // LANES):
        part = field[:, half * LANES : (half + 1) * LANES]
        slabs[slot + half, 0:lon_count, :] = part
        slabs[slot + half, lon_count : 2 * lon_count, :] = part


def near_kernel(sides, shifts, basis_ids, values, own, beside, summed, slabs):
    lon_count, channels = own.shape
    halves = channels // LANES
    fill_twice(slabs, 0, own[...].astype(F32))
    fill_twice(slabs, halves, beside[...].astype(F32))
    summed[...] = jnp.zeros_like(summed)

    def add_entry(entry, carry):
        source = (sides[0, entry] - 1) * halves
        target = basis_ids[0, entry] * halves
        shift = shifts[0, entry]
        value = values[0, entry]

        @pl.when(source >= 0)
        def _():
            for half in range(halves):
                summed[target + half] += value * slabs[source + half, pl.ds(shift, lon_count), :]

        return carry

    lax.fori_loop(0, sides.shape[1], add_entry, 0)


def mix_kernel(
    sides, shifts, basis_ids, values, distant, summed_in, weights_hbm, cotangent_hbm,
    activated_hbm, grad_pre, partial_w_hbm, summed,
    slabs, basis, preact, weights, cotangent, activated, partial_w, arrived, left,
):
    del summed_in
    lon_count, channels = distant.shape
    halves = channels // LANES
    basis_count = weights.shape[0] // channels
    get_weights = pltpu.make_async_copy(weights_hbm, weights, arrived.at[0])
    get_cotangent = pltpu.make_async_copy(cotangent_hbm, cotangent, arrived.at[1])
    get_weights.start()
    get_cotangent.start()
    fill_twice(slabs, 0, distant[...].astype(F32))

    def add_entry(entry, carry):
        target = basis_ids[0, entry] * halves
        shift = shifts[0, entry]
        value = values[0, entry]

        @pl.when(sides[0, entry] == 0)
        def _():
            for half in range(halves):
                summed[target + half] += value * slabs[half, pl.ds(shift, lon_count), :]

        return carry

    lax.fori_loop(0, sides.shape[1], add_entry, 0)
    for column in range(basis_count * halves):
        basis[:, column * LANES : (column + 1) * LANES] = summed[column].astype(BF16)
    get_weights.wait()
    preact[...] = jnp.dot(basis[...], weights[...], preferred_element_type=F32)
    get_cotangent.wait()

    def gelu_rows(step, carry):
        rows = pl.ds(pl.multiple_of(step * SLAB, SLAB), SLAB)
        v = preact[rows, :]
        root = math.sqrt(2.0 / math.pi)
        square = v * v
        bent = jnp.tanh(root * (v + 0.044715 * (v * square)))
        activated[rows, :] = (0.5 * v * (1.0 + bent)).astype(BF16)
        slope = 0.5 * (1.0 + bent) + 0.5 * v * (1.0 - bent * bent) * (
            root * (1.0 + (3.0 * 0.044715) * square)
        )
        grad_pre[rows, :] = (cotangent[rows, :].astype(F32) * slope).astype(BF16)
        return carry

    lax.fori_loop(0, lon_count // SLAB, gelu_rows, 0)
    put = [pltpu.make_async_copy(activated, activated_hbm, left.at[basis_count])]
    put[0].start()
    for k in range(basis_count):
        rows = slice(k * channels, (k + 1) * channels)
        partial_w[rows, :] = lax.dot_general(
            basis[:, rows], grad_pre[...], (((0,), (0,)), ((), ())), preferred_element_type=F32
        ).astype(BF16)
        put.append(
            pltpu.make_async_copy(partial_w.at[rows], partial_w_hbm.at[rows], left.at[k])
        )
        put[-1].start()
    for copy in put:
        copy.wait()


def backward_kernel(
    sides, shifts, basis_ids, values, grad_pre, weights, distant, own, beside, slabs, summed,
):
    lon_count, channels = grad_pre.shape
    halves = channels // LANES
    basis_count = weights.shape[0] // channels
    for k in range(basis_count):
        product = lax.dot_general(
            grad_pre[...],
            weights[k * channels : (k + 1) * channels, :],
            (((1,), (1,)), ((), ())),
            preferred_element_type=F32,
        )
        fill_twice(slabs, k * halves, product.astype(BF16).astype(F32))
    summed[...] = jnp.zeros_like(summed)

    def add_entry(entry, carry):
        target = sides[0, entry] * halves
        source = basis_ids[0, entry] * halves
        start = lon_count - shifts[0, entry]
        value = values[0, entry]
        for half in range(halves):
            summed[target + half] += value * slabs[source + half, pl.ds(start, lon_count), :]
        return carry

    lax.fori_loop(0, sides.shape[1], add_entry, 0)
    for slot, out in enumerate((distant, own, beside)):
        for half in range(halves):
            out[:, half * LANES : (half + 1) * LANES] = summed[slot * halves + half].astype(out.dtype)


def sum_kernel(scale, pieces, after, out):
    del after
    total = pieces[0].astype(F32)
    for i in range(1, pieces.shape[0]):
        total = total + pieces[i].astype(F32)
    total = (total * scale).astype(BF16)
    for i in range(out.shape[0]):
        out[i] = total


def specs(scalars, arrays, outside=0):
    return (
        [pl.BlockSpec(memory_space=pltpu.SMEM)] * scalars
        + [pl.BlockSpec(memory_space=pltpu.VMEM)] * arrays
        + [pl.BlockSpec(memory_space=pltpu.HBM)] * outside
    )


def params():
    return pltpu.CompilerParams(vmem_limit_bytes=VMEM_BYTES)


def shape(dims, dtype):
    return jax.ShapeDtypeStruct(dims, dtype)


def near_terms(tables, own, beside, wide):
    lon_count, channels = own.shape
    return pl.pallas_call(
        near_kernel,
        out_shape=shape((wide // LANES, lon_count, LANES), F32),
        in_specs=specs(4, 2),
        out_specs=specs(0, 1)[0],
        scratch_shapes=[pltpu.VMEM((2 * channels // LANES, 2 * lon_count, LANES), F32)],
        compiler_params=params(),
        cost_estimate=pl.CostEstimate(flops=0, bytes_accessed=8 << 20, transcendentals=0),
        name="near_terms",
    )(*tables, own, beside)


def mix(tables, distant, summed, weights, cotangent):
    lon_count, channels = distant.shape
    wide = weights.shape[0]
    return pl.pallas_call(
        mix_kernel,
        out_shape=(
            shape((lon_count, channels), BF16),
            shape((lon_count, channels), BF16),
            shape((wide, channels), BF16),
            shape(summed.shape, F32),
        ),
        in_specs=specs(4, 2, 2),
        out_specs=tuple(specs(0, 0, 1) + specs(0, 1) + specs(0, 0, 1) + specs(0, 1)),
        input_output_aliases={5: 3},
        scratch_shapes=[
            pltpu.VMEM((channels // LANES, 2 * lon_count, LANES), F32),
            pltpu.VMEM((lon_count, wide), BF16),
            pltpu.VMEM((lon_count, channels), F32),
            pltpu.VMEM((wide, channels), BF16),
            pltpu.VMEM((lon_count, channels), BF16),
            pltpu.VMEM((lon_count, channels), BF16),
            pltpu.VMEM((wide, channels), BF16),
            pltpu.SemaphoreType.DMA((2,)),
            pltpu.SemaphoreType.DMA((wide // channels + 1,)),
        ],
        compiler_params=params(),
        cost_estimate=pl.CostEstimate(
            flops=4 * lon_count * wide * channels, bytes_accessed=8 << 20, transcendentals=0
        ),
        name="mix",
    )(*tables, distant, summed, weights, cotangent)[:3]


def backward(tables, grad_pre, weights):
    lon_count, channels = grad_pre.shape
    halves = channels // LANES
    wide = weights.shape[0]
    return pl.pallas_call(
        backward_kernel,
        out_shape=(
            shape((lon_count, channels), BF16),
            shape((lon_count, channels), F32),
            shape((lon_count, channels), BF16),
        ),
        in_specs=specs(4, 2),
        out_specs=tuple(specs(0, 3)),
        scratch_shapes=[
            pltpu.VMEM((wide // LANES, 2 * lon_count, LANES), F32),
            pltpu.VMEM((3 * halves, lon_count, LANES), F32),
        ],
        compiler_params=params(),
        cost_estimate=pl.CostEstimate(
            flops=2 * lon_count * wide * channels, bytes_accessed=8 << 20, transcendentals=0
        ),
        name="backward",
    )(*tables, grad_pre, weights)


def summed_copies(pieces, count, scale, after):
    return pl.pallas_call(
        functools.partial(sum_kernel, scale),
        out_shape=shape((count,) + pieces.shape[1:], BF16),
        in_specs=specs(0, 1) + [pl.BlockSpec(memory_space=pl.ANY)],
        out_specs=specs(0, 1)[0],
        compiler_params=params(),
        name="summed_copies",
    )(pieces, after)


def on_device(inputs, cotangent, weights, cycle_offsets, lon_shifts, basis_ids, entry_values):
    own = inputs[0, 0]
    lon_count, channels = own.shape
    basis_count = weights.shape[0]
    wide = basis_count * channels
    flat_weights = weights.reshape(wide, channels)
    off_chip, on_chip = pair_swap(LAT, 1), pair_swap(LAT, 0)
    sides = 1 + cycle_offsets * (1 - 2 * lax.axis_index("core"))
    tables = (sides, lon_shifts, basis_ids, entry_values.astype(F32))
    distant = lax.ppermute(own, LAT, off_chip)
    beside = lax.ppermute(own, LAT, on_chip)
    summed = near_terms(tables, own, beside, wide)
    activated, grad_pre, partial_w = mix(tables, distant, summed, flat_weights, cotangent[0, 0])

    near, far = lax.axis_size(NEAR), lax.axis_size(FAR)
    pieces = lax.all_to_all(partial_w.reshape(near, -1, channels), NEAR, 0, 0)
    to_distant, middle, to_beside = backward(tables, grad_pre, flat_weights)
    from_distant = lax.ppermute(to_distant, LAT, off_chip)
    from_beside = lax.ppermute(to_beside, LAT, on_chip)
    field_gradient = (middle + from_distant.astype(F32) + from_beside.astype(F32)).astype(BF16)

    cell_count = lax.axis_size(LAT) * lax.axis_size(ENS) * lon_count
    copies = summed_copies(pieces, far, 1.0, to_beside)
    pieces = lax.all_to_all(copies, FAR, 0, 0)
    copies = summed_copies(pieces, near, 1.0 / math.sqrt(cell_count), field_gradient)
    whole = lax.all_to_all(copies, NEAR, 0, 0)
    grad_weights = whole.reshape(basis_count, channels, channels).astype(F32)
    return (activated[None, None], field_gradient[None, None], grad_weights)


def solution(mesh):
    lat_count, ens_count = mesh.devices.shape
    grid = Mesh(
        np.asarray(mesh.devices).reshape(lat_count // 4, 2, 2, 4, ens_count // 4),
        LAT + ENS,
    )
    placed = (
        P(ENS, LAT, None, None),
        P(ENS, LAT, None, None),
        P(),
        P(LAT, None),
        P(LAT, None),
        P(LAT, None),
        P(LAT, None),
    )
    return jax.shard_map(
        on_device,
        mesh=grid,
        in_specs=placed,
        out_specs=(P(ENS, LAT, None, None), P(ENS, LAT, None, None), P()),
        check_vma=False,
    )
```

```python
import math

import jax
import jax.numpy as jnp
import numpy as np
from jax import lax
from jax.experimental import pallas as pl
from jax.experimental.pallas import tpu as pltpu
from jax.sharding import Mesh
from jax.sharding import PartitionSpec as P

BF16 = jnp.bfloat16
F32 = jnp.float32
LANES = 128
SLAB = 48
PARTS = 3
VMEM_BYTES = 48 * 1024 * 1024
LAT = ("za", "zp", "core")
ENS = ("x", "y")
NEAR = ("zp", "core", "x", "y")
FAR = ("za",)


def pair_swap(axis, first):
    devices = range(lax.axis_size(axis))
    pairs = [(i, i + 1) for i in devices if i % 2 == first and i + 1 in devices]
    return pairs + [(j, i) for i, j in pairs]


def fill_twice(slabs, slot, field):
    lon_count = field.shape[0]
    for half in range(field.shape[1] // LANES):
        part = field[:, half * LANES : (half + 1) * LANES]
        slabs[slot + half, 0:lon_count, :] = part
        slabs[slot + half, lon_count : 2 * lon_count, :] = part


def fetched(tables, held, arrived):
    copies = [pltpu.make_async_copy(t, h, arrived.at[i]) for i, (t, h) in enumerate(zip(tables, held))]
    for copy in copies:
        copy.start()
    return copies


def spread(values, rows):
    count = values.shape[1]
    wide = jnp.broadcast_to(values[...].astype(F32), (count, count))
    row = lax.broadcasted_iota(jnp.int32, (count, count), 0)
    column = lax.broadcasted_iota(jnp.int32, (count, count), 1)
    picked = jnp.sum(jnp.where(row == column, wide, 0.0), axis=1, keepdims=True)
    rows[...] = jnp.broadcast_to(picked, rows.shape)


def add_rows(total, source, value, halves, target, slot, start):
    lon_count = total.shape[1]
    for half in range(halves):
        total[target + half] += value * source[slot + half, pl.ds(start, lon_count), :]


def own_kernel(
    offsets_hbm, shifts_hbm, basis_ids_hbm, values, own_hbm, summed, coefs,
    offsets, shifts, basis_ids, own, slabs, arrived,
):
    halves = own.shape[1] // LANES
    copies = fetched(
        (offsets_hbm, shifts_hbm, basis_ids_hbm, own_hbm), (offsets, shifts, basis_ids, own), arrived
    )
    spread(values, coefs)
    summed[...] = jnp.zeros_like(summed)
    for copy in copies:
        copy.wait()
    fill_twice(slabs, 0, own[...].astype(F32))

    def add_entry(entry, carry):
        @pl.when(offsets[0, entry] == 0)
        def _():
            add_rows(
                summed, slabs, coefs[pl.ds(entry, 1), :], halves,
                basis_ids[0, entry] * halves, 0, shifts[0, entry],
            )

        return carry

    lax.fori_loop(0, offsets.shape[1], add_entry, 0)


def mix_kernel(
    offsets_hbm, shifts_hbm, basis_ids_hbm, coefs, beside, distant, summed_in, weights_hbm, cotangent_hbm,
    activated_hbm, grad_pre, partial_w_hbm, summed,
    offsets, shifts, basis_ids, slabs, basis, weights, cotangent, activated, partial_w,
    arrived, left,
):
    del summed_in
    lon_count, channels = distant.shape
    halves = channels // LANES
    basis_count = weights.shape[0] // channels
    copies = fetched(
        (offsets_hbm, shifts_hbm, basis_ids_hbm, weights_hbm, cotangent_hbm),
        (offsets, shifts, basis_ids, weights, cotangent),
        arrived,
    )
    for copy in copies[:3]:
        copy.wait()
    fill_twice(slabs, 0, distant[...].astype(F32))
    fill_twice(slabs, halves, beside[...].astype(F32))
    turn = 1 - 2 * lax.axis_index("core")

    def add_entry(entry, carry):
        side = offsets[0, entry] * turn

        @pl.when(side != 0)
        def _():
            add_rows(
                summed, slabs, coefs[pl.ds(entry, 1), :], halves,
                basis_ids[0, entry] * halves, (side + 1) // 2 * halves, shifts[0, entry],
            )

        return carry

    lax.fori_loop(0, offsets.shape[1], add_entry, 0)
    copies[3].wait()
    copies[4].wait()
    root = math.sqrt(2.0 / math.pi)
    part = lon_count // PARTS
    for first in range(0, lon_count, part):
        rows = slice(first, first + part)
        for column in range(basis_count * halves):
            basis[rows, column * LANES : (column + 1) * LANES] = summed[column, rows, :].astype(BF16)
        preact = jnp.dot(basis[rows, :], weights[...], preferred_element_type=F32)
        for slab in range(0, part, SLAB):
            v = preact[slab : slab + SLAB]
            inner = slice(first + slab, first + slab + SLAB)
            square = v * v
            bent = jnp.tanh(v * (root + (root * 0.044715) * square))
            half_sum = 0.5 + 0.5 * bent
            activated[inner, :] = (v * half_sum).astype(BF16)
            slope = half_sum + (v * (0.5 - 0.5 * (bent * bent))) * (
                root + (3.0 * 0.044715 * root) * square
            )
            grad_pre[inner, :] = (cotangent[inner, :].astype(F32) * slope).astype(BF16)
    put = [pltpu.make_async_copy(activated, activated_hbm, left.at[basis_count])]
    put[0].start()
    for k in range(basis_count):
        rows = slice(k * channels, (k + 1) * channels)
        partial_w[rows, :] = lax.dot_general(
            basis[:, rows], grad_pre[...], (((0,), (0,)), ((), ())), preferred_element_type=F32
        ).astype(BF16)
        put.append(
            pltpu.make_async_copy(partial_w.at[rows], partial_w_hbm.at[rows], left.at[k])
        )
        put[-1].start()
    for copy in put:
        copy.wait()


def backward_kernel(
    offsets_hbm, shifts_hbm, basis_ids_hbm, coefs, grad_pre, weights_hbm, distant, own, beside,
    offsets, shifts, basis_ids, weights, slabs, summed, arrived,
):
    lon_count, channels = grad_pre.shape
    halves = channels // LANES
    basis_count = weights.shape[0] // channels
    copies = fetched(
        (offsets_hbm, shifts_hbm, basis_ids_hbm, weights_hbm),
        (offsets, shifts, basis_ids, weights),
        arrived,
    )
    summed[...] = jnp.zeros_like(summed)
    for copy in copies:
        copy.wait()
    for k in range(basis_count):
        product = lax.dot_general(
            grad_pre[...],
            weights[k * channels : (k + 1) * channels, :],
            (((1,), (1,)), ((), ())),
            preferred_element_type=F32,
        )
        fill_twice(slabs, k * halves, product.astype(BF16).astype(F32))
    turn = 1 - 2 * lax.axis_index("core")

    def add_entry(entry, carry):
        add_rows(
            summed, slabs, coefs[pl.ds(entry, 1), :], halves,
            (offsets[0, entry] * turn + 1) * halves, basis_ids[0, entry] * halves,
            lon_count - shifts[0, entry],
        )
        return carry

    lax.fori_loop(0, offsets.shape[1], add_entry, 0)
    for slot, out in enumerate((distant, own, beside)):
        for half in range(halves):
            out[:, half * LANES : (half + 1) * LANES] = summed[slot * halves + half].astype(out.dtype)


def vmem():
    return pl.BlockSpec(memory_space=pltpu.VMEM)


def hbm():
    return pl.BlockSpec(memory_space=pltpu.HBM)


def kept_out(arrays):
    return [pltpu.with_memory_space_constraint(array, pltpu.HBM) for array in arrays]


def params():
    return pltpu.CompilerParams(vmem_limit_bytes=VMEM_BYTES)


def cost(flops, mib):
    return pl.CostEstimate(flops=flops, bytes_accessed=mib << 20, transcendentals=0)


def shape(dims, dtype):
    return jax.ShapeDtypeStruct(dims, dtype)


def table_scratch(entry_count):
    return [pltpu.SMEM((1, entry_count), jnp.int32)] * 3


def own_terms(tables, values, own, wide):
    lon_count, channels = own.shape
    entry_count = values.shape[1]
    return pl.pallas_call(
        own_kernel,
        out_shape=(
            shape((wide // LANES, lon_count, LANES), F32),
            shape((entry_count, LANES), F32),
        ),
        in_specs=[hbm()] * 3 + [vmem(), hbm()],
        out_specs=(vmem(), vmem()),
        scratch_shapes=table_scratch(entry_count)
        + [
            pltpu.VMEM((lon_count, channels), BF16),
            pltpu.VMEM((channels // LANES, 2 * lon_count, LANES), F32),
            pltpu.SemaphoreType.DMA((4,)),
        ],
        compiler_params=params(),
        cost_estimate=cost(0, 4),
        name="own_terms",
    )(*kept_out(tables), values, *kept_out([own]))


def mix(tables, coefs, distant, beside, summed, weights, cotangent):
    lon_count, channels = distant.shape
    wide = weights.shape[0]
    field = pltpu.VMEM((lon_count, channels), BF16)
    square = pltpu.VMEM((wide, channels), BF16)
    return pl.pallas_call(
        mix_kernel,
        out_shape=(
            shape((lon_count, channels), BF16),
            shape((lon_count, channels), BF16),
            shape((wide, channels), BF16),
            shape(summed.shape, F32),
        ),
        in_specs=[hbm()] * 3 + [vmem()] * 4 + [hbm()] * 2,
        out_specs=(hbm(), vmem(), hbm(), vmem()),
        input_output_aliases={6: 3},
        scratch_shapes=table_scratch(coefs.shape[0])
        + [
            pltpu.VMEM((2 * channels // LANES, 2 * lon_count, LANES), F32),
            pltpu.VMEM((lon_count, wide), BF16),
            square,
            field,
            field,
            square,
            pltpu.SemaphoreType.DMA((5,)),
            pltpu.SemaphoreType.DMA((wide // channels + 1,)),
        ],
        compiler_params=params(),
        cost_estimate=cost(4 * lon_count * wide * channels, 8),
        name="mix",
    )(*kept_out(tables), coefs, beside, distant, summed, *kept_out([weights, cotangent]))[:3]


def backward(tables, coefs, grad_pre, weights):
    lon_count, channels = grad_pre.shape
    halves = channels // LANES
    wide = weights.shape[0]
    return pl.pallas_call(
        backward_kernel,
        out_shape=(
            shape((lon_count, channels), BF16),
            shape((lon_count, channels), F32),
            shape((lon_count, channels), BF16),
        ),
        in_specs=[hbm()] * 3 + [vmem()] * 2 + [hbm()],
        out_specs=(vmem(), vmem(), vmem()),
        scratch_shapes=table_scratch(coefs.shape[0])
        + [
            pltpu.VMEM((wide, channels), BF16),
            pltpu.VMEM((wide // LANES, 2 * lon_count, LANES), F32),
            pltpu.VMEM((3 * halves, lon_count, LANES), F32),
            pltpu.SemaphoreType.DMA((4,)),
        ],
        compiler_params=params(),
        cost_estimate=cost(2 * lon_count * wide * channels, 8),
        name="backward",
    )(*kept_out(tables), coefs, grad_pre, *kept_out([weights]))


def to_all(block, axes):
    count = lax.axis_size(axes)
    return lax.all_to_all(jnp.broadcast_to(block[None], (count,) + block.shape), axes, 0, 0)


def on_device(inputs, cotangent, weights, cycle_offsets, lon_shifts, basis_ids, entry_values):
    own = inputs[0, 0]
    lon_count, channels = own.shape
    basis_count = weights.shape[0]
    wide = basis_count * channels
    flat_weights = weights.reshape(wide, channels)
    off_chip, on_chip = pair_swap(LAT, 1), pair_swap(LAT, 0)
    tables = (cycle_offsets, lon_shifts, basis_ids)
    distant = lax.ppermute(own, LAT, off_chip)
    beside = lax.ppermute(own, LAT, on_chip)
    summed, coefs = own_terms(tables, entry_values, own, wide)
    activated, grad_pre, partial_w = mix(
        tables, coefs, distant, beside, summed, flat_weights, cotangent[0, 0]
    )

    pieces = lax.all_to_all(
        partial_w.reshape(lax.axis_size(NEAR), -1, channels), NEAR, 0, 0
    )
    to_distant, middle, to_beside = backward(tables, coefs, grad_pre, flat_weights)
    from_distant = lax.ppermute(to_distant, LAT, off_chip)
    from_beside = lax.ppermute(to_beside, LAT, on_chip)
    chunk = pieces.astype(F32).sum(0).astype(BF16)
    chunk, _ = lax.optimization_barrier((chunk, to_beside))
    pieces = to_all(chunk, FAR)
    field_gradient = (middle + from_distant.astype(F32) + from_beside.astype(F32)).astype(BF16)
    cell_count = lax.axis_size(LAT) * lax.axis_size(ENS) * lon_count
    chunk = (pieces.astype(F32).sum(0) * (1.0 / math.sqrt(cell_count))).astype(BF16)
    chunk, field_gradient = lax.optimization_barrier((chunk, field_gradient))
    pieces = to_all(chunk, NEAR)
    grad_weights = pieces.reshape(weights.shape).astype(F32)
    return (activated[None, None], field_gradient[None, None], grad_weights)


def solution(mesh):
    lat_count, ens_count = mesh.devices.shape
    grid = Mesh(
        np.asarray(mesh.devices).reshape(lat_count // 4, 2, 2, 4, ens_count // 4),
        LAT + ENS,
    )
    placed = (
        P(ENS, LAT, None, None),
        P(ENS, LAT, None, None),
        P(),
        P(LAT, None),
        P(LAT, None),
        P(LAT, None),
        P(LAT, None),
    )
    return jax.shard_map(
        on_device,
        mesh=grid,
        in_specs=placed,
        out_specs=(P(ENS, LAT, None, None), P(ENS, LAT, None, None), P()),
        check_vma=False,
    )
```

```python
import math

import jax
import jax.numpy as jnp
import numpy as np
from jax import lax
from jax.experimental import pallas as pl
from jax.experimental.pallas import tpu as pltpu
from jax.sharding import Mesh
from jax.sharding import PartitionSpec as P

BF16 = jnp.bfloat16
F32 = jnp.float32
LANES = 128
SLAB = 48
PARTS = 5
TOGETHER = 4
ENTRY_UNIT = 1 << 16
SLOT_UNIT = 1 << 12
PLAN = 128
VMEM_BYTES = 48 * 1024 * 1024
LAT = ("za", "zp", "core")
ENS = ("x", "y")
NEAR = ("zp", "core", "x", "y")
FAR = ("za",)


def pair_swap(axis, first):
    devices = range(lax.axis_size(axis))
    pairs = [(i, i + 1) for i in devices if i % 2 == first and i + 1 in devices]
    return pairs + [(j, i) for i, j in pairs]


def fill_twice(slabs, slot, field):
    lon_count = field.shape[0]
    for half in range(field.shape[1] // LANES):
        part = field[:, half * LANES : (half + 1) * LANES]
        slabs[slot + half, 0:lon_count, :] = part
        slabs[slot + half, lon_count : 2 * lon_count, :] = part


def fetched(tables, held, arrived):
    copies = [pltpu.make_async_copy(t, h, arrived.at[i]) for i, (t, h) in enumerate(zip(tables, held))]
    for copy in copies:
        copy.start()
    return copies


def spread(values, rows):
    count = values.shape[1]
    wide = jnp.broadcast_to(values[...].astype(F32), (count, count))
    row = lax.broadcasted_iota(jnp.int32, (count, count), 0)
    column = lax.broadcasted_iota(jnp.int32, (count, count), 1)
    picked = jnp.sum(jnp.where(row == column, wide, 0.0), axis=1, keepdims=True)
    rows[...] = jnp.zeros_like(rows)
    rows[0:count, :] = jnp.broadcast_to(picked, (count, rows.shape[1]))


def list_room(entry_count):
    return -(-entry_count // TOGETHER) * TOGETHER


def plan_entries(plan, offsets, shifts, basis_ids, lon_count, basis_count):
    entry_count = offsets.shape[1]
    room = list_room(entry_count)
    groups = basis_count + 3
    counts = groups * room

    def clear(i, carry):
        plan[0, i] = jnp.where(i < counts, entry_count * ENTRY_UNIT, 0)
        return carry

    lax.fori_loop(0, counts + groups, clear, 0)
    turn = 1 - 2 * lax.axis_index("core")

    def note(group, code):
        place = plan[0, counts + group]
        plan[0, group * room + place] = code
        plan[0, counts + group] = place + 1

    def add_entry(entry, carry):
        side = offsets[0, entry] * turn
        basis = basis_ids[0, entry]
        shift = shifts[0, entry]

        @pl.when(side != 0)
        def _():
            slot = jnp.where(side > 0, SLOT_UNIT, 0)
            note(basis, entry * ENTRY_UNIT + slot + shift)

        note(basis_count + 1 + side, entry * ENTRY_UNIT + basis * SLOT_UNIT + lon_count - shift)
        return carry

    lax.fori_loop(0, entry_count, add_entry, 0)


def passes_of(plan, group, groups, room):
    return (plan[0, groups * room + group] + (TOGETHER - 1)) // TOGETHER


def few_terms(plan, first, coefs, slabs, lon_count, halves):
    terms = [None] * halves
    for i in range(TOGETHER):
        code = plan[0, first + i]
        entry = lax.shift_right_logical(code, 16)
        slot = (lax.shift_right_logical(code, 12) & 15) * halves
        start = code & (SLOT_UNIT - 1)
        value = coefs[pl.ds(entry, 1), :]
        for half in range(halves):
            term = value * slabs[slot + half, pl.ds(start, lon_count), :]
            terms[half] = term if i == 0 else terms[half] + term
    return terms


def add_rows(total, source, value, halves, target, slot, start):
    lon_count = total.shape[1]
    for half in range(halves):
        total[target + half] += value * source[slot + half, pl.ds(start, lon_count), :]


def own_kernel(
    offsets_hbm, shifts_hbm, basis_ids_hbm, values, own_hbm, weights_hbm, cotangent_hbm,
    summed, coefs, plan_out, weights, cotangent,
    offsets, shifts, basis_ids, plan, own, slabs, arrived, left,
):
    halves = own.shape[1] // LANES
    copies = fetched(
        (offsets_hbm, shifts_hbm, basis_ids_hbm, own_hbm, weights_hbm, cotangent_hbm),
        (offsets, shifts, basis_ids, own, weights, cotangent),
        arrived,
    )
    spread(values, coefs)
    summed[...] = jnp.zeros_like(summed)
    for copy in copies[:4]:
        copy.wait()
    plan_entries(
        plan, offsets, shifts, basis_ids, own.shape[0], summed.shape[0] // halves
    )
    put_plan = pltpu.make_async_copy(plan, plan_out, left)
    put_plan.start()
    fill_twice(slabs, 0, own[...].astype(F32))

    def add_entry(entry, carry):
        @pl.when(offsets[0, entry] == 0)
        def _():
            add_rows(
                summed, slabs, coefs[pl.ds(entry, 1), :], halves,
                basis_ids[0, entry] * halves, 0, shifts[0, entry],
            )

        return carry

    lax.fori_loop(0, offsets.shape[1], add_entry, 0)
    put_plan.wait()
    for copy in copies[4:]:
        copy.wait()


def mix_kernel(
    plan_in, coefs, beside, distant, summed_in, weights, cotangent,
    activated_hbm, grad_pre, partial_w_hbm, summed,
    plan, slabs, basis, activated, partial_w, arrived, left,
):
    del summed_in
    lon_count, channels = distant.shape
    halves = channels // LANES
    basis_count = weights.shape[0] // channels
    get_plan = pltpu.make_async_copy(plan_in, plan, arrived)
    get_plan.start()
    fill_twice(slabs, 0, distant[...].astype(F32))
    fill_twice(slabs, halves, beside[...].astype(F32))
    get_plan.wait()
    groups, room = basis_count + 3, list_room(coefs.shape[0] - 8)
    for k in range(basis_count):
        passes = passes_of(plan, k, groups, room)

        def add_pass(i, carry):
            terms = few_terms(plan, k * room + i * TOGETHER, coefs, slabs, lon_count, halves)
            for half in range(halves):
                summed[k * halves + half] += terms[half]
            return carry

        last = jnp.maximum(passes - 1, 0)
        lax.fori_loop(0, last, add_pass, 0)
        terms = few_terms(plan, k * room + last * TOGETHER, coefs, slabs, lon_count, halves)
        for half in range(halves):
            column = k * halves + half
            basis[:, column * LANES : (column + 1) * LANES] = (summed[column] + terms[half]).astype(BF16)
    root = math.sqrt(2.0 / math.pi)
    part = lon_count // PARTS
    for first in range(0, lon_count, part):
        rows = slice(first, first + part)
        preact = jnp.dot(basis[rows, :], weights[...], preferred_element_type=F32)
        for slab in range(0, part, SLAB):
            v = preact[slab : slab + SLAB]
            inner = slice(first + slab, first + slab + SLAB)
            square = v * v
            bent = jnp.tanh(v * (root + (root * 0.044715) * square))
            half_sum = 0.5 + 0.5 * bent
            activated[inner, :] = (v * half_sum).astype(BF16)
            slope = half_sum + (v * (0.5 - 0.5 * (bent * bent))) * (
                root + (3.0 * 0.044715 * root) * square
            )
            grad_pre[inner, :] = (cotangent[inner, :].astype(F32) * slope).astype(BF16)
    put = [pltpu.make_async_copy(activated, activated_hbm, left.at[basis_count])]
    put[0].start()
    for k in range(basis_count):
        rows = slice(k * channels, (k + 1) * channels)
        partial_w[rows, :] = lax.dot_general(
            basis[:, rows], grad_pre[...], (((0,), (0,)), ((), ())), preferred_element_type=F32
        ).astype(BF16)
        put.append(
            pltpu.make_async_copy(partial_w.at[rows], partial_w_hbm.at[rows], left.at[k])
        )
        put[-1].start()
    for copy in put:
        copy.wait()


def backward_kernel(
    plan_in, coefs, grad_pre, weights, distant, own, beside,
    plan, slabs, summed, arrived,
):
    lon_count, channels = grad_pre.shape
    halves = channels // LANES
    basis_count = weights.shape[0] // channels
    get_plan = pltpu.make_async_copy(plan_in, plan, arrived)
    get_plan.start()
    for k in range(basis_count):
        product = lax.dot_general(
            grad_pre[...],
            weights[k * channels : (k + 1) * channels, :],
            (((1,), (1,)), ((), ())),
            preferred_element_type=F32,
        )
        fill_twice(slabs, k * halves, product.astype(BF16).astype(F32))
    get_plan.wait()
    groups, room = basis_count + 3, list_room(coefs.shape[0] - 8)
    for side, out in enumerate((distant, own, beside)):
        group = basis_count + side
        passes = passes_of(plan, group, groups, room)

        def terms_of(i):
            return few_terms(plan, group * room + i * TOGETHER, coefs, slabs, lon_count, halves)

        def put(terms):
            for half in range(halves):
                out[:, half * LANES : (half + 1) * LANES] = terms[half].astype(out.dtype)

        @pl.when(passes <= 1)
        def _():
            put(terms_of(0))

        @pl.when(passes > 1)
        def _():
            for half, term in enumerate(terms_of(0)):
                summed[half] = term

            def add_pass(i, carry):
                for half, term in enumerate(terms_of(i)):
                    summed[half] += term
                return carry

            lax.fori_loop(1, passes - 1, add_pass, 0)
            put([summed[half] + term for half, term in enumerate(terms_of(passes - 1))])


def vmem():
    return pl.BlockSpec(memory_space=pltpu.VMEM)


def hbm():
    return pl.BlockSpec(memory_space=pltpu.HBM)


def kept_out(arrays):
    return [pltpu.with_memory_space_constraint(array, pltpu.HBM) for array in arrays]


def either():
    return pl.BlockSpec(memory_space=pl.ANY)


def params():
    return pltpu.CompilerParams(vmem_limit_bytes=VMEM_BYTES)


def cost(flops, mib):
    return pl.CostEstimate(flops=flops, bytes_accessed=mib << 20, transcendentals=0)


def shape(dims, dtype):
    return jax.ShapeDtypeStruct(dims, dtype)


def table_scratch(entry_count):
    return [pltpu.SMEM((1, entry_count), jnp.int32)] * 3


def own_terms(tables, values, own, weights, cotangent):
    lon_count, channels = own.shape
    wide = weights.shape[0]
    entry_count = values.shape[1]
    return pl.pallas_call(
        own_kernel,
        out_shape=(
            shape((wide // LANES, lon_count, LANES), F32),
            shape((entry_count + 8, LANES), F32),
            shape((1, PLAN), jnp.int32),
            shape(weights.shape, BF16),
            shape(cotangent.shape, BF16),
        ),
        in_specs=[hbm()] * 3 + [vmem()] + [hbm()] * 3,
        out_specs=(vmem(), vmem(), either(), vmem(), vmem()),
        scratch_shapes=[pltpu.SMEM((1, entry_count), jnp.int32)] * 3
        + [
            pltpu.SMEM((1, PLAN), jnp.int32),
            pltpu.VMEM((lon_count, channels), BF16),
            pltpu.VMEM((channels // LANES, 2 * lon_count, LANES), F32),
            pltpu.SemaphoreType.DMA((6,)),
            pltpu.SemaphoreType.DMA,
        ],
        compiler_params=params(),
        cost_estimate=cost(0, 4),
        name="own_terms",
    )(*kept_out(tables), values, *kept_out([own, weights, cotangent]))


def mix(plan, coefs, distant, beside, summed, weights, cotangent):
    lon_count, channels = distant.shape
    wide = weights.shape[0]
    field = pltpu.VMEM((lon_count, channels), BF16)
    square = pltpu.VMEM((wide, channels), BF16)
    return pl.pallas_call(
        mix_kernel,
        out_shape=(
            shape((lon_count, channels), BF16),
            shape((lon_count, channels), BF16),
            shape((wide, channels), BF16),
            shape(summed.shape, F32),
        ),
        in_specs=[either()] + [vmem()] * 6,
        out_specs=(hbm(), vmem(), hbm(), vmem()),
        input_output_aliases={4: 3},
        scratch_shapes=[
            pltpu.SMEM((1, PLAN), jnp.int32),
            pltpu.VMEM((2 * channels // LANES, 2 * lon_count, LANES), F32),
            pltpu.VMEM((lon_count, wide), BF16),
            field,
            square,
            pltpu.SemaphoreType.DMA,
            pltpu.SemaphoreType.DMA((wide // channels + 1,)),
        ],
        compiler_params=params(),
        cost_estimate=cost(4 * lon_count * wide * channels, 8),
        name="mix",
    )(plan, coefs, beside, distant, summed, weights, cotangent)[:3]


def backward(plan, coefs, grad_pre, weights):
    lon_count, channels = grad_pre.shape
    wide = weights.shape[0]
    return pl.pallas_call(
        backward_kernel,
        out_shape=(
            shape((lon_count, channels), BF16),
            shape((lon_count, channels), F32),
            shape((lon_count, channels), BF16),
        ),
        in_specs=[either()] + [vmem()] * 3,
        out_specs=(vmem(), vmem(), vmem()),
        scratch_shapes=[
            pltpu.SMEM((1, PLAN), jnp.int32),
            pltpu.VMEM((wide // LANES, 2 * lon_count, LANES), F32),
            pltpu.VMEM((channels // LANES, lon_count, LANES), F32),
            pltpu.SemaphoreType.DMA,
        ],
        compiler_params=params(),
        cost_estimate=cost(2 * lon_count * wide * channels, 8),
        name="backward",
    )(plan, coefs, grad_pre, weights)


def to_all(block, axes):
    count = lax.axis_size(axes)
    return lax.all_to_all(jnp.broadcast_to(block[None], (count,) + block.shape), axes, 0, 0)


def on_device(inputs, cotangent, weights, cycle_offsets, lon_shifts, basis_ids, entry_values):
    own = inputs[0, 0]
    lon_count, channels = own.shape
    basis_count = weights.shape[0]
    wide = basis_count * channels
    off_chip, on_chip = pair_swap(LAT, 1), pair_swap(LAT, 0)
    tables = (cycle_offsets, lon_shifts, basis_ids)
    distant = lax.ppermute(own, LAT, off_chip)
    beside = lax.ppermute(own, LAT, on_chip)
    summed, coefs, plan, flat_weights, cotangent = own_terms(
        tables, entry_values, own, weights.reshape(wide, channels), cotangent[0, 0]
    )
    activated, grad_pre, partial_w = mix(
        plan, coefs, distant, beside, summed, flat_weights, cotangent
    )

    pieces = lax.all_to_all(
        partial_w.reshape(lax.axis_size(NEAR), -1, channels), NEAR, 0, 0
    )
    to_distant, middle, to_beside = backward(plan, coefs, grad_pre, flat_weights)
    from_distant = lax.ppermute(to_distant, LAT, off_chip)
    from_beside = lax.ppermute(to_beside, LAT, on_chip)
    chunk = pieces.astype(F32).sum(0).astype(BF16)
    chunk, _ = lax.optimization_barrier((chunk, to_beside))
    pieces = to_all(chunk, FAR)
    field_gradient = (middle + from_distant.astype(F32) + from_beside.astype(F32)).astype(BF16)
    cell_count = lax.axis_size(LAT) * lax.axis_size(ENS) * lon_count
    chunk = (pieces.astype(F32).sum(0) * (1.0 / math.sqrt(cell_count))).astype(BF16)
    chunk, field_gradient = lax.optimization_barrier((chunk, field_gradient))
    pieces = to_all(chunk, NEAR)
    grad_weights = pieces.reshape(weights.shape).astype(F32)
    return (activated[None, None], field_gradient[None, None], grad_weights)


def solution(mesh):
    lat_count, ens_count = mesh.devices.shape
    grid = Mesh(
        np.asarray(mesh.devices).reshape(lat_count // 4, 2, 2, 4, ens_count // 4),
        LAT + ENS,
    )
    placed = (
        P(ENS, LAT, None, None),
        P(ENS, LAT, None, None),
        P(),
        P(LAT, None),
        P(LAT, None),
        P(LAT, None),
        P(LAT, None),
    )
    return jax.shard_map(
        on_device,
        mesh=grid,
        in_specs=placed,
        out_specs=(P(ENS, LAT, None, None), P(ENS, LAT, None, None), P()),
        check_vma=False,
    )
```

```python
import math

import jax
import jax.numpy as jnp
import numpy as np
from jax import lax
from jax.experimental import pallas as pl
from jax.experimental.pallas import tpu as pltpu
from jax.sharding import Mesh
from jax.sharding import PartitionSpec as P

BF16 = jnp.bfloat16
F32 = jnp.float32
LANES = 128
SLAB = 48
PARTS = 5
TOGETHER = 4
ENTRY_UNIT = 1 << 16
SLOT_UNIT = 1 << 12
PLAN = 128
VMEM_BYTES = 48 * 1024 * 1024
LAT = ("za", "zp", "core")
ENS = ("x", "y")
NEAR = ("x", "y", "zp", "core")
FAR = ("za",)


def pair_swap(axis, first):
    devices = range(lax.axis_size(axis))
    pairs = [(i, i + 1) for i in devices if i % 2 == first and i + 1 in devices]
    return pairs + [(j, i) for i, j in pairs]


def fill_twice(slabs, slot, field):
    lon_count = field.shape[0]
    for half in range(field.shape[1] // LANES):
        part = field[:, half * LANES : (half + 1) * LANES]
        slabs[slot + half, 0:lon_count, :] = part
        slabs[slot + half, lon_count : 2 * lon_count, :] = part


def fetched(tables, held, arrived):
    copies = [pltpu.make_async_copy(t, h, arrived.at[i]) for i, (t, h) in enumerate(zip(tables, held))]
    for copy in copies:
        copy.start()
    return copies


def spread(values, rows):
    count = values.shape[1]
    wide = jnp.broadcast_to(values[...].astype(F32), (count, count))
    row = lax.broadcasted_iota(jnp.int32, (count, count), 0)
    column = lax.broadcasted_iota(jnp.int32, (count, count), 1)
    picked = jnp.sum(jnp.where(row == column, wide, 0.0), axis=1, keepdims=True)
    rows[...] = jnp.zeros_like(rows)
    rows[0:count, :] = jnp.broadcast_to(picked, (count, rows.shape[1]))


def list_room(entry_count):
    return -(-entry_count // TOGETHER) * TOGETHER


def plan_entries(plan, offsets, shifts, basis_ids, lon_count, basis_count):
    entry_count = offsets.shape[1]
    room = list_room(entry_count)
    groups = basis_count + 3
    counts = groups * room

    def clear(i, carry):
        plan[0, i] = jnp.where(i < counts, entry_count * ENTRY_UNIT, 0)
        return carry

    lax.fori_loop(0, counts + groups, clear, 0)
    turn = 1 - 2 * lax.axis_index("core")

    def note(group, code):
        place = plan[0, counts + group]
        plan[0, group * room + place] = code
        plan[0, counts + group] = place + 1

    def add_entry(entry, carry):
        side = offsets[0, entry] * turn
        basis = basis_ids[0, entry]
        shift = shifts[0, entry]

        @pl.when(side != 0)
        def _():
            slot = jnp.where(side > 0, SLOT_UNIT, 0)
            note(basis, entry * ENTRY_UNIT + slot + shift)

        note(basis_count + 1 + side, entry * ENTRY_UNIT + basis * SLOT_UNIT + lon_count - shift)
        return carry

    lax.fori_loop(0, entry_count, add_entry, 0)


def passes_of(plan, group, groups, room):
    return (plan[0, groups * room + group] + (TOGETHER - 1)) // TOGETHER


def few_terms(plan, first, coefs, slabs, lon_count, halves):
    terms = [None] * halves
    for i in range(TOGETHER):
        code = plan[0, first + i]
        entry = lax.shift_right_logical(code, 16)
        slot = (lax.shift_right_logical(code, 12) & 15) * halves
        start = code & (SLOT_UNIT - 1)
        value = coefs[pl.ds(entry, 1), :]
        for half in range(halves):
            term = value * slabs[slot + half, pl.ds(start, lon_count), :]
            terms[half] = term if i == 0 else terms[half] + term
    return terms


def add_rows(total, source, value, halves, target, slot, start):
    lon_count = total.shape[1]
    for half in range(halves):
        total[target + half] += value * source[slot + half, pl.ds(start, lon_count), :]


def own_kernel(
    offsets_hbm, shifts_hbm, basis_ids_hbm, values, own_hbm, weights_hbm, cotangent_hbm,
    summed, coefs, plan_out, weights, cotangent,
    offsets, shifts, basis_ids, plan, own, slabs, arrived, left,
):
    halves = own.shape[1] // LANES
    copies = fetched(
        (offsets_hbm, shifts_hbm, basis_ids_hbm, own_hbm, weights_hbm, cotangent_hbm),
        (offsets, shifts, basis_ids, own, weights, cotangent),
        arrived,
    )
    spread(values, coefs)
    summed[...] = jnp.zeros_like(summed)
    for copy in copies[:4]:
        copy.wait()
    plan_entries(
        plan, offsets, shifts, basis_ids, own.shape[0], summed.shape[0] // halves
    )
    put_plan = pltpu.make_async_copy(plan, plan_out, left)
    put_plan.start()
    fill_twice(slabs, 0, own[...].astype(F32))

    def add_entry(entry, carry):
        @pl.when(offsets[0, entry] == 0)
        def _():
            add_rows(
                summed, slabs, coefs[pl.ds(entry, 1), :], halves,
                basis_ids[0, entry] * halves, 0, shifts[0, entry],
            )

        return carry

    lax.fori_loop(0, offsets.shape[1], add_entry, 0)
    put_plan.wait()
    for copy in copies[4:]:
        copy.wait()


def mix_kernel(
    plan_in, coefs, beside, distant, summed_in, weights, cotangent,
    activated_hbm, grad_pre, partial_w_hbm, summed,
    plan, slabs, basis, activated, partial_w, arrived, left,
):
    del summed_in
    lon_count, channels = distant.shape
    halves = channels // LANES
    basis_count = weights.shape[0] // channels
    get_plan = pltpu.make_async_copy(plan_in, plan, arrived)
    get_plan.start()
    fill_twice(slabs, 0, distant[...].astype(F32))
    fill_twice(slabs, halves, beside[...].astype(F32))
    get_plan.wait()
    groups, room = basis_count + 3, list_room(coefs.shape[0] - 8)
    for k in range(basis_count):
        passes = passes_of(plan, k, groups, room)

        def add_pass(i, carry):
            terms = few_terms(plan, k * room + i * TOGETHER, coefs, slabs, lon_count, halves)
            for half in range(halves):
                summed[k * halves + half] += terms[half]
            return carry

        last = jnp.maximum(passes - 1, 0)
        lax.fori_loop(0, last, add_pass, 0)
        terms = few_terms(plan, k * room + last * TOGETHER, coefs, slabs, lon_count, halves)
        for half in range(halves):
            column = k * halves + half
            basis[:, column * LANES : (column + 1) * LANES] = (summed[column] + terms[half]).astype(BF16)
    root = math.sqrt(2.0 / math.pi)
    part = lon_count // PARTS
    for first in range(0, lon_count, part):
        rows = slice(first, first + part)
        preact = jnp.dot(basis[rows, :], weights[...], preferred_element_type=F32)
        for slab in range(0, part, SLAB):
            v = preact[slab : slab + SLAB]
            inner = slice(first + slab, first + slab + SLAB)
            square = v * v
            bent = jnp.tanh(v * (root + (root * 0.044715) * square))
            half_sum = 0.5 + 0.5 * bent
            activated[inner, :] = (v * half_sum).astype(BF16)
            slope = half_sum + (v * (0.5 - 0.5 * (bent * bent))) * (
                root + (3.0 * 0.044715 * root) * square
            )
            grad_pre[inner, :] = (cotangent[inner, :].astype(F32) * slope).astype(BF16)
    put = [pltpu.make_async_copy(activated, activated_hbm, left.at[basis_count])]
    put[0].start()
    for k in range(basis_count):
        rows = slice(k * channels, (k + 1) * channels)
        partial_w[rows, :] = lax.dot_general(
            basis[:, rows], grad_pre[...], (((0,), (0,)), ((), ())), preferred_element_type=F32
        ).astype(BF16)
        put.append(
            pltpu.make_async_copy(partial_w.at[rows], partial_w_hbm.at[rows], left.at[k])
        )
        put[-1].start()
    for copy in put:
        copy.wait()


def backward_kernel(
    plan_in, coefs, grad_pre, weights, distant, own, beside,
    plan, slabs, summed, arrived,
):
    lon_count, channels = grad_pre.shape
    halves = channels // LANES
    basis_count = weights.shape[0] // channels
    get_plan = pltpu.make_async_copy(plan_in, plan, arrived)
    get_plan.start()
    for k in range(basis_count):
        product = lax.dot_general(
            grad_pre[...],
            weights[k * channels : (k + 1) * channels, :],
            (((1,), (1,)), ((), ())),
            preferred_element_type=F32,
        )
        fill_twice(slabs, k * halves, product.astype(BF16).astype(F32))
    get_plan.wait()
    groups, room = basis_count + 3, list_room(coefs.shape[0] - 8)
    for side, out in enumerate((distant, own, beside)):
        group = basis_count + side
        passes = passes_of(plan, group, groups, room)

        def terms_of(i):
            return few_terms(plan, group * room + i * TOGETHER, coefs, slabs, lon_count, halves)

        def put(terms):
            for half in range(halves):
                out[:, half * LANES : (half + 1) * LANES] = terms[half].astype(out.dtype)

        @pl.when(passes <= 1)
        def _():
            put(terms_of(0))

        @pl.when(passes > 1)
        def _():
            for half, term in enumerate(terms_of(0)):
                summed[half] = term

            def add_pass(i, carry):
                for half, term in enumerate(terms_of(i)):
                    summed[half] += term
                return carry

            lax.fori_loop(1, passes - 1, add_pass, 0)
            put([summed[half] + term for half, term in enumerate(terms_of(passes - 1))])


def vmem():
    return pl.BlockSpec(memory_space=pltpu.VMEM)


def hbm():
    return pl.BlockSpec(memory_space=pltpu.HBM)


def kept_out(arrays):
    return [pltpu.with_memory_space_constraint(array, pltpu.HBM) for array in arrays]


def either():
    return pl.BlockSpec(memory_space=pl.ANY)


def params():
    return pltpu.CompilerParams(vmem_limit_bytes=VMEM_BYTES)


def cost(flops, mib):
    return pl.CostEstimate(flops=flops, bytes_accessed=mib << 20, transcendentals=0)


def shape(dims, dtype):
    return jax.ShapeDtypeStruct(dims, dtype)


def table_scratch(entry_count):
    return [pltpu.SMEM((1, entry_count), jnp.int32)] * 3


def own_terms(tables, values, own, weights, cotangent):
    lon_count, channels = own.shape
    wide = weights.shape[0]
    entry_count = values.shape[1]
    return pl.pallas_call(
        own_kernel,
        out_shape=(
            shape((wide // LANES, lon_count, LANES), F32),
            shape((entry_count + 8, LANES), F32),
            shape((1, PLAN), jnp.int32),
            shape(weights.shape, BF16),
            shape(cotangent.shape, BF16),
        ),
        in_specs=[hbm()] * 3 + [vmem()] + [hbm()] * 3,
        out_specs=(vmem(), vmem(), either(), vmem(), vmem()),
        scratch_shapes=[pltpu.SMEM((1, entry_count), jnp.int32)] * 3
        + [
            pltpu.SMEM((1, PLAN), jnp.int32),
            pltpu.VMEM((lon_count, channels), BF16),
            pltpu.VMEM((channels // LANES, 2 * lon_count, LANES), F32),
            pltpu.SemaphoreType.DMA((6,)),
            pltpu.SemaphoreType.DMA,
        ],
        compiler_params=params(),
        cost_estimate=cost(0, 4),
        name="own_terms",
    )(*kept_out(tables), values, *kept_out([own, weights, cotangent]))


def mix(plan, coefs, distant, beside, summed, weights, cotangent):
    lon_count, channels = distant.shape
    wide = weights.shape[0]
    field = pltpu.VMEM((lon_count, channels), BF16)
    square = pltpu.VMEM((wide, channels), BF16)
    return pl.pallas_call(
        mix_kernel,
        out_shape=(
            shape((lon_count, channels), BF16),
            shape((lon_count, channels), BF16),
            shape((wide, channels), BF16),
            shape(summed.shape, F32),
        ),
        in_specs=[either()] + [vmem()] * 6,
        out_specs=(hbm(), vmem(), hbm(), vmem()),
        input_output_aliases={4: 3},
        scratch_shapes=[
            pltpu.SMEM((1, PLAN), jnp.int32),
            pltpu.VMEM((2 * channels // LANES, 2 * lon_count, LANES), F32),
            pltpu.VMEM((lon_count, wide), BF16),
            field,
            square,
            pltpu.SemaphoreType.DMA,
            pltpu.SemaphoreType.DMA((wide // channels + 1,)),
        ],
        compiler_params=params(),
        cost_estimate=cost(4 * lon_count * wide * channels, 8),
        name="mix",
    )(plan, coefs, beside, distant, summed, weights, cotangent)[:3]


def backward(plan, coefs, grad_pre, weights):
    lon_count, channels = grad_pre.shape
    wide = weights.shape[0]
    return pl.pallas_call(
        backward_kernel,
        out_shape=(
            shape((lon_count, channels), BF16),
            shape((lon_count, channels), F32),
            shape((lon_count, channels), BF16),
        ),
        in_specs=[either()] + [vmem()] * 3,
        out_specs=(vmem(), vmem(), vmem()),
        scratch_shapes=[
            pltpu.SMEM((1, PLAN), jnp.int32),
            pltpu.VMEM((wide // LANES, 2 * lon_count, LANES), F32),
            pltpu.VMEM((channels // LANES, lon_count, LANES), F32),
            pltpu.SemaphoreType.DMA,
        ],
        compiler_params=params(),
        cost_estimate=cost(2 * lon_count * wide * channels, 8),
        name="backward",
    )(plan, coefs, grad_pre, weights)


def to_all(block, axes):
    count = lax.axis_size(axes)
    return lax.all_to_all(jnp.broadcast_to(block[None], (count,) + block.shape), axes, 0, 0)


def on_device(inputs, cotangent, weights, cycle_offsets, lon_shifts, basis_ids, entry_values):
    own = inputs[0, 0]
    lon_count, channels = own.shape
    basis_count = weights.shape[0]
    wide = basis_count * channels
    off_chip, on_chip = pair_swap(LAT, 1), pair_swap(LAT, 0)
    tables = (cycle_offsets, lon_shifts, basis_ids)
    distant = lax.ppermute(own, LAT, off_chip)
    beside = lax.ppermute(own, LAT, on_chip)
    summed, coefs, plan, flat_weights, cotangent = own_terms(
        tables, entry_values, own, weights.reshape(wide, channels), cotangent[0, 0]
    )
    activated, grad_pre, partial_w = mix(
        plan, coefs, distant, beside, summed, flat_weights, cotangent
    )

    pieces = lax.all_to_all(
        partial_w.reshape(lax.axis_size(NEAR), -1, channels), NEAR, 0, 0
    )
    to_distant, middle, to_beside = backward(plan, coefs, grad_pre, flat_weights)
    from_distant = lax.ppermute(to_distant, LAT, off_chip)
    from_beside = lax.ppermute(to_beside, LAT, on_chip)
    chunk = pieces.astype(F32).sum(0).astype(BF16)
    chunk, _ = lax.optimization_barrier((chunk, to_beside))
    pieces = to_all(chunk, FAR)
    field_gradient = (middle + from_distant.astype(F32) + from_beside.astype(F32)).astype(BF16)
    cell_count = lax.axis_size(LAT) * lax.axis_size(ENS) * lon_count
    chunk = (pieces.astype(F32).sum(0) * (1.0 / math.sqrt(cell_count))).astype(BF16)
    chunk, field_gradient = lax.optimization_barrier((chunk, field_gradient))
    pieces = to_all(chunk, NEAR)
    grad_weights = pieces.reshape(weights.shape).astype(F32)
    return (activated[None, None], field_gradient[None, None], grad_weights)


def solution(mesh):
    lat_count, ens_count = mesh.devices.shape
    grid = Mesh(
        np.asarray(mesh.devices).reshape(lat_count // 4, 2, 2, 4, ens_count // 4),
        LAT + ENS,
    )
    placed = (
        P(ENS, LAT, None, None),
        P(ENS, LAT, None, None),
        P(),
        P(LAT, None),
        P(LAT, None),
        P(LAT, None),
        P(LAT, None),
    )
    return jax.shard_map(
        on_device,
        mesh=grid,
        in_specs=placed,
        out_specs=(P(ENS, LAT, None, None), P(ENS, LAT, None, None), P()),
        check_vma=False,
    )
```

```python
import math

import jax
import jax.numpy as jnp
import numpy as np
from jax import lax
from jax.experimental import pallas as pl
from jax.experimental.pallas import tpu as pltpu
from jax.sharding import Mesh
from jax.sharding import PartitionSpec as P

BF16 = jnp.bfloat16
F32 = jnp.float32
LANES = 128
SLAB = 48
PARTS = 5
TOGETHER = 4
ENTRY_UNIT = 1 << 16
SLOT_UNIT = 1 << 12
PLAN = 128
VMEM_BYTES = 48 * 1024 * 1024
LAT = ("za", "zp", "core")
ENS = ("x", "y")
NEAR = ("core", "zp", "x", "y")
FAR = ("za",)


def pair_swap(axis, first):
    devices = range(lax.axis_size(axis))
    pairs = [(i, i + 1) for i in devices if i % 2 == first and i + 1 in devices]
    return pairs + [(j, i) for i, j in pairs]


def fill_twice(slabs, slot, field):
    lon_count = field.shape[0]
    for half in range(field.shape[1] // LANES):
        part = field[:, half * LANES : (half + 1) * LANES]
        slabs[slot + half, 0:lon_count, :] = part
        slabs[slot + half, lon_count : 2 * lon_count, :] = part


def fetched(tables, held, arrived):
    copies = [pltpu.make_async_copy(t, h, arrived.at[i]) for i, (t, h) in enumerate(zip(tables, held))]
    for copy in copies:
        copy.start()
    return copies


def spread(values, rows):
    count = values.shape[1]
    wide = jnp.broadcast_to(values[...].astype(F32), (count, count))
    row = lax.broadcasted_iota(jnp.int32, (count, count), 0)
    column = lax.broadcasted_iota(jnp.int32, (count, count), 1)
    picked = jnp.sum(jnp.where(row == column, wide, 0.0), axis=1, keepdims=True)
    rows[...] = jnp.zeros_like(rows)
    rows[0:count, :] = jnp.broadcast_to(picked, (count, rows.shape[1]))


def list_room(entry_count):
    return -(-entry_count // TOGETHER) * TOGETHER


def plan_entries(plan, offsets, shifts, basis_ids, lon_count, basis_count):
    entry_count = offsets.shape[1]
    room = list_room(entry_count)
    groups = basis_count + 3
    counts = groups * room

    def clear(i, carry):
        plan[0, i] = jnp.where(i < counts, entry_count * ENTRY_UNIT, 0)
        return carry

    lax.fori_loop(0, counts + groups, clear, 0)
    turn = 1 - 2 * lax.axis_index("core")

    def note(group, code):
        place = plan[0, counts + group]
        plan[0, group * room + place] = code
        plan[0, counts + group] = place + 1

    def add_entry(entry, carry):
        side = offsets[0, entry] * turn
        basis = basis_ids[0, entry]
        shift = shifts[0, entry]

        @pl.when(side != 0)
        def _():
            slot = jnp.where(side > 0, SLOT_UNIT, 0)
            note(basis, entry * ENTRY_UNIT + slot + shift)

        note(basis_count + 1 + side, entry * ENTRY_UNIT + basis * SLOT_UNIT + lon_count - shift)
        return carry

    lax.fori_loop(0, entry_count, add_entry, 0)


def passes_of(plan, group, groups, room):
    return (plan[0, groups * room + group] + (TOGETHER - 1)) // TOGETHER


def few_terms(plan, first, coefs, slabs, lon_count, halves):
    terms = [None] * halves
    for i in range(TOGETHER):
        code = plan[0, first + i]
        entry = lax.shift_right_logical(code, 16)
        slot = (lax.shift_right_logical(code, 12) & 15) * halves
        start = code & (SLOT_UNIT - 1)
        value = coefs[pl.ds(entry, 1), :]
        for half in range(halves):
            term = value * slabs[slot + half, pl.ds(start, lon_count), :]
            terms[half] = term if i == 0 else terms[half] + term
    return terms


def add_rows(total, source, value, halves, target, slot, start):
    lon_count = total.shape[1]
    for half in range(halves):
        total[target + half] += value * source[slot + half, pl.ds(start, lon_count), :]


def own_kernel(
    offsets_hbm, shifts_hbm, basis_ids_hbm, values, own_hbm, weights_hbm, cotangent_hbm,
    summed, coefs, plan_out, weights, cotangent,
    offsets, shifts, basis_ids, plan, own, slabs, arrived, left,
):
    halves = own.shape[1] // LANES
    copies = fetched(
        (offsets_hbm, shifts_hbm, basis_ids_hbm, own_hbm, weights_hbm, cotangent_hbm),
        (offsets, shifts, basis_ids, own, weights, cotangent),
        arrived,
    )
    spread(values, coefs)
    summed[...] = jnp.zeros_like(summed)
    for copy in copies[:4]:
        copy.wait()
    plan_entries(
        plan, offsets, shifts, basis_ids, own.shape[0], summed.shape[0] // halves
    )
    put_plan = pltpu.make_async_copy(plan, plan_out, left)
    put_plan.start()
    fill_twice(slabs, 0, own[...].astype(F32))

    def add_entry(entry, carry):
        @pl.when(offsets[0, entry] == 0)
        def _():
            add_rows(
                summed, slabs, coefs[pl.ds(entry, 1), :], halves,
                basis_ids[0, entry] * halves, 0, shifts[0, entry],
            )

        return carry

    lax.fori_loop(0, offsets.shape[1], add_entry, 0)
    put_plan.wait()
    for copy in copies[4:]:
        copy.wait()


def mix_kernel(
    plan_in, coefs, beside, distant, summed_in, weights, cotangent,
    activated_hbm, grad_pre, partial_w_hbm, summed,
    plan, slabs, basis, activated, partial_w, arrived, left,
):
    del summed_in
    lon_count, channels = distant.shape
    halves = channels // LANES
    basis_count = weights.shape[0] // channels
    get_plan = pltpu.make_async_copy(plan_in, plan, arrived)
    get_plan.start()
    fill_twice(slabs, 0, distant[...].astype(F32))
    fill_twice(slabs, halves, beside[...].astype(F32))
    get_plan.wait()
    groups, room = basis_count + 3, list_room(coefs.shape[0] - 8)
    for k in range(basis_count):
        passes = passes_of(plan, k, groups, room)

        def add_pass(i, carry):
            terms = few_terms(plan, k * room + i * TOGETHER, coefs, slabs, lon_count, halves)
            for half in range(halves):
                summed[k * halves + half] += terms[half]
            return carry

        last = jnp.maximum(passes - 1, 0)
        lax.fori_loop(0, last, add_pass, 0)
        terms = few_terms(plan, k * room + last * TOGETHER, coefs, slabs, lon_count, halves)
        for half in range(halves):
            column = k * halves + half
            basis[:, column * LANES : (column + 1) * LANES] = (summed[column] + terms[half]).astype(BF16)
    root = math.sqrt(2.0 / math.pi)
    part = lon_count // PARTS
    for first in range(0, lon_count, part):
        rows = slice(first, first + part)
        preact = jnp.dot(basis[rows, :], weights[...], preferred_element_type=F32)
        for slab in range(0, part, SLAB):
            v = preact[slab : slab + SLAB]
            inner = slice(first + slab, first + slab + SLAB)
            square = v * v
            bent = jnp.tanh(v * (root + (root * 0.044715) * square))
            half_sum = 0.5 + 0.5 * bent
            activated[inner, :] = (v * half_sum).astype(BF16)
            slope = half_sum + (v * (0.5 - 0.5 * (bent * bent))) * (
                root + (3.0 * 0.044715 * root) * square
            )
            grad_pre[inner, :] = (cotangent[inner, :].astype(F32) * slope).astype(BF16)
    put = [pltpu.make_async_copy(activated, activated_hbm, left.at[basis_count])]
    put[0].start()
    for k in range(basis_count):
        rows = slice(k * channels, (k + 1) * channels)
        partial_w[rows, :] = lax.dot_general(
            basis[:, rows], grad_pre[...], (((0,), (0,)), ((), ())), preferred_element_type=F32
        ).astype(BF16)
        put.append(
            pltpu.make_async_copy(partial_w.at[rows], partial_w_hbm.at[rows], left.at[k])
        )
        put[-1].start()
    for copy in put:
        copy.wait()


def backward_kernel(
    plan_in, coefs, grad_pre, weights, distant, own, beside,
    plan, slabs, summed, arrived,
):
    lon_count, channels = grad_pre.shape
    halves = channels // LANES
    basis_count = weights.shape[0] // channels
    get_plan = pltpu.make_async_copy(plan_in, plan, arrived)
    get_plan.start()
    for k in range(basis_count):
        product = lax.dot_general(
            grad_pre[...],
            weights[k * channels : (k + 1) * channels, :],
            (((1,), (1,)), ((), ())),
            preferred_element_type=F32,
        )
        fill_twice(slabs, k * halves, product.astype(BF16).astype(F32))
    get_plan.wait()
    groups, room = basis_count + 3, list_room(coefs.shape[0] - 8)
    for side, out in enumerate((distant, own, beside)):
        group = basis_count + side
        passes = passes_of(plan, group, groups, room)

        def terms_of(i):
            return few_terms(plan, group * room + i * TOGETHER, coefs, slabs, lon_count, halves)

        def put(terms):
            for half in range(halves):
                out[:, half * LANES : (half + 1) * LANES] = terms[half].astype(out.dtype)

        @pl.when(passes <= 1)
        def _():
            put(terms_of(0))

        @pl.when(passes > 1)
        def _():
            for half, term in enumerate(terms_of(0)):
                summed[half] = term

            def add_pass(i, carry):
                for half, term in enumerate(terms_of(i)):
                    summed[half] += term
                return carry

            lax.fori_loop(1, passes - 1, add_pass, 0)
            put([summed[half] + term for half, term in enumerate(terms_of(passes - 1))])


def vmem():
    return pl.BlockSpec(memory_space=pltpu.VMEM)


def hbm():
    return pl.BlockSpec(memory_space=pltpu.HBM)


def kept_out(arrays):
    return [pltpu.with_memory_space_constraint(array, pltpu.HBM) for array in arrays]


def either():
    return pl.BlockSpec(memory_space=pl.ANY)


def params():
    return pltpu.CompilerParams(vmem_limit_bytes=VMEM_BYTES)


def cost(flops, mib):
    return pl.CostEstimate(flops=flops, bytes_accessed=mib << 20, transcendentals=0)


def shape(dims, dtype):
    return jax.ShapeDtypeStruct(dims, dtype)


def table_scratch(entry_count):
    return [pltpu.SMEM((1, entry_count), jnp.int32)] * 3


def own_terms(tables, values, own, weights, cotangent):
    lon_count, channels = own.shape
    wide = weights.shape[0]
    entry_count = values.shape[1]
    return pl.pallas_call(
        own_kernel,
        out_shape=(
            shape((wide // LANES, lon_count, LANES), F32),
            shape((entry_count + 8, LANES), F32),
            shape((1, PLAN), jnp.int32),
            shape(weights.shape, BF16),
            shape(cotangent.shape, BF16),
        ),
        in_specs=[hbm()] * 3 + [vmem()] + [hbm()] * 3,
        out_specs=(vmem(), vmem(), either(), vmem(), vmem()),
        scratch_shapes=[pltpu.SMEM((1, entry_count), jnp.int32)] * 3
        + [
            pltpu.SMEM((1, PLAN), jnp.int32),
            pltpu.VMEM((lon_count, channels), BF16),
            pltpu.VMEM((channels // LANES, 2 * lon_count, LANES), F32),
            pltpu.SemaphoreType.DMA((6,)),
            pltpu.SemaphoreType.DMA,
        ],
        compiler_params=params(),
        cost_estimate=cost(0, 4),
        name="own_terms",
    )(*kept_out(tables), values, *kept_out([own, weights, cotangent]))


def mix(plan, coefs, distant, beside, summed, weights, cotangent):
    lon_count, channels = distant.shape
    wide = weights.shape[0]
    field = pltpu.VMEM((lon_count, channels), BF16)
    square = pltpu.VMEM((wide, channels), BF16)
    return pl.pallas_call(
        mix_kernel,
        out_shape=(
            shape((lon_count, channels), BF16),
            shape((lon_count, channels), BF16),
            shape((wide, channels), BF16),
            shape(summed.shape, F32),
        ),
        in_specs=[either()] + [vmem()] * 6,
        out_specs=(hbm(), vmem(), hbm(), vmem()),
        input_output_aliases={4: 3},
        scratch_shapes=[
            pltpu.SMEM((1, PLAN), jnp.int32),
            pltpu.VMEM((2 * channels // LANES, 2 * lon_count, LANES), F32),
            pltpu.VMEM((lon_count, wide), BF16),
            field,
            square,
            pltpu.SemaphoreType.DMA,
            pltpu.SemaphoreType.DMA((wide // channels + 1,)),
        ],
        compiler_params=params(),
        cost_estimate=cost(4 * lon_count * wide * channels, 8),
        name="mix",
    )(plan, coefs, beside, distant, summed, weights, cotangent)[:3]


def backward(plan, coefs, grad_pre, weights):
    lon_count, channels = grad_pre.shape
    wide = weights.shape[0]
    return pl.pallas_call(
        backward_kernel,
        out_shape=(
            shape((lon_count, channels), BF16),
            shape((lon_count, channels), F32),
            shape((lon_count, channels), BF16),
        ),
        in_specs=[either()] + [vmem()] * 3,
        out_specs=(vmem(), vmem(), vmem()),
        scratch_shapes=[
            pltpu.SMEM((1, PLAN), jnp.int32),
            pltpu.VMEM((wide // LANES, 2 * lon_count, LANES), F32),
            pltpu.VMEM((channels // LANES, lon_count, LANES), F32),
            pltpu.SemaphoreType.DMA,
        ],
        compiler_params=params(),
        cost_estimate=cost(2 * lon_count * wide * channels, 8),
        name="backward",
    )(plan, coefs, grad_pre, weights)


def to_all(block, axes):
    count = lax.axis_size(axes)
    return lax.all_to_all(jnp.broadcast_to(block[None], (count,) + block.shape), axes, 0, 0)


def on_device(inputs, cotangent, weights, cycle_offsets, lon_shifts, basis_ids, entry_values):
    own = inputs[0, 0]
    lon_count, channels = own.shape
    basis_count = weights.shape[0]
    wide = basis_count * channels
    off_chip, on_chip = pair_swap(LAT, 1), pair_swap(LAT, 0)
    tables = (cycle_offsets, lon_shifts, basis_ids)
    distant = lax.ppermute(own, LAT, off_chip)
    beside = lax.ppermute(own, LAT, on_chip)
    summed, coefs, plan, flat_weights, cotangent = own_terms(
        tables, entry_values, own, weights.reshape(wide, channels), cotangent[0, 0]
    )
    activated, grad_pre, partial_w = mix(
        plan, coefs, distant, beside, summed, flat_weights, cotangent
    )

    pieces = lax.all_to_all(
        partial_w.reshape(lax.axis_size(NEAR), -1, channels), NEAR, 0, 0
    )
    to_distant, middle, to_beside = backward(plan, coefs, grad_pre, flat_weights)
    from_distant = lax.ppermute(to_distant, LAT, off_chip)
    from_beside = lax.ppermute(to_beside, LAT, on_chip)
    chunk = pieces.astype(F32).sum(0).astype(BF16)
    chunk, _ = lax.optimization_barrier((chunk, to_beside))
    pieces = to_all(chunk, FAR)
    field_gradient = (middle + from_distant.astype(F32) + from_beside.astype(F32)).astype(BF16)
    cell_count = lax.axis_size(LAT) * lax.axis_size(ENS) * lon_count
    chunk = (pieces.astype(F32).sum(0) * (1.0 / math.sqrt(cell_count))).astype(BF16)
    chunk, field_gradient = lax.optimization_barrier((chunk, field_gradient))
    pieces = to_all(chunk, NEAR)
    grad_weights = pieces.reshape(weights.shape).astype(F32)
    return (activated[None, None], field_gradient[None, None], grad_weights)


def solution(mesh):
    lat_count, ens_count = mesh.devices.shape
    grid = Mesh(
        np.asarray(mesh.devices).reshape(lat_count // 4, 2, 2, 4, ens_count // 4),
        LAT + ENS,
    )
    placed = (
        P(ENS, LAT, None, None),
        P(ENS, LAT, None, None),
        P(),
        P(LAT, None),
        P(LAT, None),
        P(LAT, None),
        P(LAT, None),
    )
    return jax.shard_map(
        on_device,
        mesh=grid,
        in_specs=placed,
        out_specs=(P(ENS, LAT, None, None), P(ENS, LAT, None, None), P()),
        check_vma=False,
    )
```

```python
import math

import jax
import jax.numpy as jnp
import numpy as np
from jax import lax
from jax.experimental import pallas as pl
from jax.experimental.pallas import tpu as pltpu
from jax.sharding import Mesh
from jax.sharding import PartitionSpec as P

BF16 = jnp.bfloat16
F32 = jnp.float32
LANES = 128
SLAB = 48
PARTS = 5
TOGETHER = 4
ENTRY_UNIT = 1 << 16
SLOT_UNIT = 1 << 12
PLAN = 128
VMEM_BYTES = 48 * 1024 * 1024
LAT = ("za", "zp", "core")
ENS = ("x", "y")
NEAR = ("zp", "core", "y", "x")
FAR = ("za",)


def pair_swap(axis, first):
    devices = range(lax.axis_size(axis))
    pairs = [(i, i + 1) for i in devices if i % 2 == first and i + 1 in devices]
    return pairs + [(j, i) for i, j in pairs]


def fill_twice(slabs, slot, field):
    lon_count = field.shape[0]
    for half in range(field.shape[1] // LANES):
        part = field[:, half * LANES : (half + 1) * LANES]
        slabs[slot + half, 0:lon_count, :] = part
        slabs[slot + half, lon_count : 2 * lon_count, :] = part


def fetched(tables, held, arrived):
    copies = [pltpu.make_async_copy(t, h, arrived.at[i]) for i, (t, h) in enumerate(zip(tables, held))]
    for copy in copies:
        copy.start()
    return copies


def spread(values, rows):
    count = values.shape[1]
    wide = jnp.broadcast_to(values[...].astype(F32), (count, count))
    row = lax.broadcasted_iota(jnp.int32, (count, count), 0)
    column = lax.broadcasted_iota(jnp.int32, (count, count), 1)
    picked = jnp.sum(jnp.where(row == column, wide, 0.0), axis=1, keepdims=True)
    rows[...] = jnp.zeros_like(rows)
    rows[0:count, :] = jnp.broadcast_to(picked, (count, rows.shape[1]))


def list_room(entry_count):
    return -(-entry_count // TOGETHER) * TOGETHER


def plan_entries(plan, offsets, shifts, basis_ids, lon_count, basis_count):
    entry_count = offsets.shape[1]
    room = list_room(entry_count)
    groups = basis_count + 3
    counts = groups * room

    def clear(i, carry):
        plan[0, i] = jnp.where(i < counts, entry_count * ENTRY_UNIT, 0)
        return carry

    lax.fori_loop(0, counts + groups, clear, 0)
    turn = 1 - 2 * lax.axis_index("core")

    def note(group, code):
        place = plan[0, counts + group]
        plan[0, group * room + place] = code
        plan[0, counts + group] = place + 1

    def add_entry(entry, carry):
        side = offsets[0, entry] * turn
        basis = basis_ids[0, entry]
        shift = shifts[0, entry]

        @pl.when(side != 0)
        def _():
            slot = jnp.where(side > 0, SLOT_UNIT, 0)
            note(basis, entry * ENTRY_UNIT + slot + shift)

        note(basis_count + 1 + side, entry * ENTRY_UNIT + basis * SLOT_UNIT + lon_count - shift)
        return carry

    lax.fori_loop(0, entry_count, add_entry, 0)


def passes_of(plan, group, groups, room):
    return (plan[0, groups * room + group] + (TOGETHER - 1)) // TOGETHER


def few_terms(plan, first, coefs, slabs, lon_count, halves):
    terms = [None] * halves
    for i in range(TOGETHER):
        code = plan[0, first + i]
        entry = lax.shift_right_logical(code, 16)
        slot = (lax.shift_right_logical(code, 12) & 15) * halves
        start = code & (SLOT_UNIT - 1)
        value = coefs[pl.ds(entry, 1), :]
        for half in range(halves):
            term = value * slabs[slot + half, pl.ds(start, lon_count), :]
            terms[half] = term if i == 0 else terms[half] + term
    return terms


def add_rows(total, source, value, halves, target, slot, start):
    lon_count = total.shape[1]
    for half in range(halves):
        total[target + half] += value * source[slot + half, pl.ds(start, lon_count), :]


def own_kernel(
    offsets_hbm, shifts_hbm, basis_ids_hbm, values, own_hbm, weights_hbm, cotangent_hbm,
    summed, coefs, plan_out, weights, cotangent,
    offsets, shifts, basis_ids, plan, own, slabs, arrived, left,
):
    halves = own.shape[1] // LANES
    copies = fetched(
        (offsets_hbm, shifts_hbm, basis_ids_hbm, own_hbm, weights_hbm, cotangent_hbm),
        (offsets, shifts, basis_ids, own, weights, cotangent),
        arrived,
    )
    spread(values, coefs)
    summed[...] = jnp.zeros_like(summed)
    for copy in copies[:4]:
        copy.wait()
    plan_entries(
        plan, offsets, shifts, basis_ids, own.shape[0], summed.shape[0] // halves
    )
    put_plan = pltpu.make_async_copy(plan, plan_out, left)
    put_plan.start()
    fill_twice(slabs, 0, own[...].astype(F32))

    def add_entry(entry, carry):
        @pl.when(offsets[0, entry] == 0)
        def _():
            add_rows(
                summed, slabs, coefs[pl.ds(entry, 1), :], halves,
                basis_ids[0, entry] * halves, 0, shifts[0, entry],
            )

        return carry

    lax.fori_loop(0, offsets.shape[1], add_entry, 0)
    put_plan.wait()
    for copy in copies[4:]:
        copy.wait()


def mix_kernel(
    plan_in, coefs, beside, distant, summed_in, weights, cotangent,
    activated_hbm, grad_pre, partial_w_hbm, summed,
    plan, slabs, basis, activated, partial_w, arrived, left,
):
    del summed_in
    lon_count, channels = distant.shape
    halves = channels // LANES
    basis_count = weights.shape[0] // channels
    get_plan = pltpu.make_async_copy(plan_in, plan, arrived)
    get_plan.start()
    fill_twice(slabs, 0, distant[...].astype(F32))
    fill_twice(slabs, halves, beside[...].astype(F32))
    get_plan.wait()
    groups, room = basis_count + 3, list_room(coefs.shape[0] - 8)
    for k in range(basis_count):
        passes = passes_of(plan, k, groups, room)

        def add_pass(i, carry):
            terms = few_terms(plan, k * room + i * TOGETHER, coefs, slabs, lon_count, halves)
            for half in range(halves):
                summed[k * halves + half] += terms[half]
            return carry

        last = jnp.maximum(passes - 1, 0)
        lax.fori_loop(0, last, add_pass, 0)
        terms = few_terms(plan, k * room + last * TOGETHER, coefs, slabs, lon_count, halves)
        for half in range(halves):
            column = k * halves + half
            basis[:, column * LANES : (column + 1) * LANES] = (summed[column] + terms[half]).astype(BF16)
    root = math.sqrt(2.0 / math.pi)
    part = lon_count // PARTS
    for first in range(0, lon_count, part):
        rows = slice(first, first + part)
        preact = jnp.dot(basis[rows, :], weights[...], preferred_element_type=F32)
        for slab in range(0, part, SLAB):
            v = preact[slab : slab + SLAB]
            inner = slice(first + slab, first + slab + SLAB)
            square = v * v
            bent = jnp.tanh(v * (root + (root * 0.044715) * square))
            half_sum = 0.5 + 0.5 * bent
            activated[inner, :] = (v * half_sum).astype(BF16)
            slope = half_sum + (v * (0.5 - 0.5 * (bent * bent))) * (
                root + (3.0 * 0.044715 * root) * square
            )
            grad_pre[inner, :] = (cotangent[inner, :].astype(F32) * slope).astype(BF16)
    put = [pltpu.make_async_copy(activated, activated_hbm, left.at[basis_count])]
    put[0].start()
    for k in range(basis_count):
        rows = slice(k * channels, (k + 1) * channels)
        partial_w[rows, :] = lax.dot_general(
            basis[:, rows], grad_pre[...], (((0,), (0,)), ((), ())), preferred_element_type=F32
        ).astype(BF16)
        put.append(
            pltpu.make_async_copy(partial_w.at[rows], partial_w_hbm.at[rows], left.at[k])
        )
        put[-1].start()
    for copy in put:
        copy.wait()


def backward_kernel(
    plan_in, coefs, grad_pre, weights, distant, own, beside,
    plan, slabs, summed, arrived,
):
    lon_count, channels = grad_pre.shape
    halves = channels // LANES
    basis_count = weights.shape[0] // channels
    get_plan = pltpu.make_async_copy(plan_in, plan, arrived)
    get_plan.start()
    for k in range(basis_count):
        product = lax.dot_general(
            grad_pre[...],
            weights[k * channels : (k + 1) * channels, :],
            (((1,), (1,)), ((), ())),
            preferred_element_type=F32,
        )
        fill_twice(slabs, k * halves, product.astype(BF16).astype(F32))
    get_plan.wait()
    groups, room = basis_count + 3, list_room(coefs.shape[0] - 8)
    for side, out in enumerate((distant, own, beside)):
        group = basis_count + side
        passes = passes_of(plan, group, groups, room)

        def terms_of(i):
            return few_terms(plan, group * room + i * TOGETHER, coefs, slabs, lon_count, halves)

        def put(terms):
            for half in range(halves):
                out[:, half * LANES : (half + 1) * LANES] = terms[half].astype(out.dtype)

        @pl.when(passes <= 1)
        def _():
            put(terms_of(0))

        @pl.when(passes > 1)
        def _():
            for half, term in enumerate(terms_of(0)):
                summed[half] = term

            def add_pass(i, carry):
                for half, term in enumerate(terms_of(i)):
                    summed[half] += term
                return carry

            lax.fori_loop(1, passes - 1, add_pass, 0)
            put([summed[half] + term for half, term in enumerate(terms_of(passes - 1))])


def vmem():
    return pl.BlockSpec(memory_space=pltpu.VMEM)


def hbm():
    return pl.BlockSpec(memory_space=pltpu.HBM)


def kept_out(arrays):
    return [pltpu.with_memory_space_constraint(array, pltpu.HBM) for array in arrays]


def either():
    return pl.BlockSpec(memory_space=pl.ANY)


def params():
    return pltpu.CompilerParams(vmem_limit_bytes=VMEM_BYTES)


def cost(flops, mib):
    return pl.CostEstimate(flops=flops, bytes_accessed=mib << 20, transcendentals=0)


def shape(dims, dtype):
    return jax.ShapeDtypeStruct(dims, dtype)


def table_scratch(entry_count):
    return [pltpu.SMEM((1, entry_count), jnp.int32)] * 3


def own_terms(tables, values, own, weights, cotangent):
    lon_count, channels = own.shape
    wide = weights.shape[0]
    entry_count = values.shape[1]
    return pl.pallas_call(
        own_kernel,
        out_shape=(
            shape((wide // LANES, lon_count, LANES), F32),
            shape((entry_count + 8, LANES), F32),
            shape((1, PLAN), jnp.int32),
            shape(weights.shape, BF16),
            shape(cotangent.shape, BF16),
        ),
        in_specs=[hbm()] * 3 + [vmem()] + [hbm()] * 3,
        out_specs=(vmem(), vmem(), either(), vmem(), vmem()),
        scratch_shapes=[pltpu.SMEM((1, entry_count), jnp.int32)] * 3
        + [
            pltpu.SMEM((1, PLAN), jnp.int32),
            pltpu.VMEM((lon_count, channels), BF16),
            pltpu.VMEM((channels // LANES, 2 * lon_count, LANES), F32),
            pltpu.SemaphoreType.DMA((6,)),
            pltpu.SemaphoreType.DMA,
        ],
        compiler_params=params(),
        cost_estimate=cost(0, 4),
        name="own_terms",
    )(*kept_out(tables), values, *kept_out([own, weights, cotangent]))


def mix(plan, coefs, distant, beside, summed, weights, cotangent):
    lon_count, channels = distant.shape
    wide = weights.shape[0]
    field = pltpu.VMEM((lon_count, channels), BF16)
    square = pltpu.VMEM((wide, channels), BF16)
    return pl.pallas_call(
        mix_kernel,
        out_shape=(
            shape((lon_count, channels), BF16),
            shape((lon_count, channels), BF16),
            shape((wide, channels), BF16),
            shape(summed.shape, F32),
        ),
        in_specs=[either()] + [vmem()] * 6,
        out_specs=(hbm(), vmem(), hbm(), vmem()),
        input_output_aliases={4: 3},
        scratch_shapes=[
            pltpu.SMEM((1, PLAN), jnp.int32),
            pltpu.VMEM((2 * channels // LANES, 2 * lon_count, LANES), F32),
            pltpu.VMEM((lon_count, wide), BF16),
            field,
            square,
            pltpu.SemaphoreType.DMA,
            pltpu.SemaphoreType.DMA((wide // channels + 1,)),
        ],
        compiler_params=params(),
        cost_estimate=cost(4 * lon_count * wide * channels, 8),
        name="mix",
    )(plan, coefs, beside, distant, summed, weights, cotangent)[:3]


def backward(plan, coefs, grad_pre, weights):
    lon_count, channels = grad_pre.shape
    wide = weights.shape[0]
    return pl.pallas_call(
        backward_kernel,
        out_shape=(
            shape((lon_count, channels), BF16),
            shape((lon_count, channels), F32),
            shape((lon_count, channels), BF16),
        ),
        in_specs=[either()] + [vmem()] * 3,
        out_specs=(vmem(), vmem(), vmem()),
        scratch_shapes=[
            pltpu.SMEM((1, PLAN), jnp.int32),
            pltpu.VMEM((wide // LANES, 2 * lon_count, LANES), F32),
            pltpu.VMEM((channels // LANES, lon_count, LANES), F32),
            pltpu.SemaphoreType.DMA,
        ],
        compiler_params=params(),
        cost_estimate=cost(2 * lon_count * wide * channels, 8),
        name="backward",
    )(plan, coefs, grad_pre, weights)


def to_all(block, axes):
    count = lax.axis_size(axes)
    return lax.all_to_all(jnp.broadcast_to(block[None], (count,) + block.shape), axes, 0, 0)


def on_device(inputs, cotangent, weights, cycle_offsets, lon_shifts, basis_ids, entry_values):
    own = inputs[0, 0]
    lon_count, channels = own.shape
    basis_count = weights.shape[0]
    wide = basis_count * channels
    off_chip, on_chip = pair_swap(LAT, 1), pair_swap(LAT, 0)
    tables = (cycle_offsets, lon_shifts, basis_ids)
    distant = lax.ppermute(own, LAT, off_chip)
    beside = lax.ppermute(own, LAT, on_chip)
    summed, coefs, plan, flat_weights, cotangent = own_terms(
        tables, entry_values, own, weights.reshape(wide, channels), cotangent[0, 0]
    )
    activated, grad_pre, partial_w = mix(
        plan, coefs, distant, beside, summed, flat_weights, cotangent
    )

    pieces = lax.all_to_all(
        partial_w.reshape(lax.axis_size(NEAR), -1, channels), NEAR, 0, 0
    )
    to_distant, middle, to_beside = backward(plan, coefs, grad_pre, flat_weights)
    from_distant = lax.ppermute(to_distant, LAT, off_chip)
    from_beside = lax.ppermute(to_beside, LAT, on_chip)
    chunk = pieces.astype(F32).sum(0).astype(BF16)
    chunk, _ = lax.optimization_barrier((chunk, to_beside))
    pieces = to_all(chunk, FAR)
    field_gradient = (middle + from_distant.astype(F32) + from_beside.astype(F32)).astype(BF16)
    cell_count = lax.axis_size(LAT) * lax.axis_size(ENS) * lon_count
    chunk = (pieces.astype(F32).sum(0) * (1.0 / math.sqrt(cell_count))).astype(BF16)
    chunk, field_gradient = lax.optimization_barrier((chunk, field_gradient))
    pieces = to_all(chunk, NEAR)
    grad_weights = pieces.reshape(weights.shape).astype(F32)
    return (activated[None, None], field_gradient[None, None], grad_weights)


def solution(mesh):
    lat_count, ens_count = mesh.devices.shape
    grid = Mesh(
        np.asarray(mesh.devices).reshape(lat_count // 4, 2, 2, 4, ens_count // 4),
        LAT + ENS,
    )
    placed = (
        P(ENS, LAT, None, None),
        P(ENS, LAT, None, None),
        P(),
        P(LAT, None),
        P(LAT, None),
        P(LAT, None),
        P(LAT, None),
    )
    return jax.shard_map(
        on_device,
        mesh=grid,
        in_specs=placed,
        out_specs=(P(ENS, LAT, None, None), P(ENS, LAT, None, None), P()),
        check_vma=False,
    )
```
